512 devices in a mesh: dp: 64 (over z_hi, y, x, core), mp: 8 (over z_lo).
Axes of the slice: x: 4, y: 4, z: 16 (z_hi: 2, z_lo: 8; z = z_hi * 8 + z_lo), core: 2. Of those that a mesh axis runs over, the one named last changes fastest.
Arguments:
- layer_input: bfloat16 [32768, 8192], P('dp', 'mp')
- norm_gain: bfloat16 [8192], P('mp'), may hold values from 0.5 to 1.5
- value_weight: bfloat16 [1024, 8192], P('dp', 'mp'), may hold values from -0.0625 to 0.0625
- value_cotangent: bfloat16 [32768, 1024], P('dp', 'mp')
- doc_ids: int32 [32768], P('dp'), may hold values from 0 to 127, never falling along the last dimension, each value on 1 to 512 neighbouring positions
- owners: int32 [64], replicated, may hold values from 0 to 63, as said below
- noise_seeds: int32 [64], replicated, may hold values from 0 to 1073741823
- master: float32 [4096, 8192], P('dp', 'mp'), may hold values from -0.12 to 0.12
- moment_one: float32 [4096, 8192], P('dp', 'mp'), may hold values from -6 to 6
- moment_two: float32 [4096, 8192], P('dp', 'mp'), may hold values from 0.5 to 8
Outputs:
- input_grad: bfloat16 [32768, 8192], P('dp', 'mp')
- new_master: float32 [4096, 8192], P('dp', 'mp')
- new_moment_one: float32 [4096, 8192], P('dp', 'mp')
- new_moment_two: float32 [4096, 8192], P('dp', 'mp')
The draws below stay inside these ranges and needn't reach their ends.
Inputs may be any that keep to these rules, and one draw needn't show every extreme that they name: `owners`: each index of dp is named by at most 4 entries, and one is named by exactly 4.
All inputs are finite; a program needn't handle non-finite values.
Results may differ from the reference program's by a relative error of at most 0.0016.
Values may be sent and summed in bfloat16 or wider, within the bound.
No kernel may reach another device: no remote copies, remote signals or barrier semaphores. Data moves between devices by JAX's collectives and lax.ppermute only.
A program may use at most 64 MiB of HBM per device.

```python
import math
import jax
import jax.numpy as jnp
import numpy as np
from jax import lax

D = 8192
KV = 1024
TOK_DEV = 512
CAP = 4
TOKENS = 32768
GROUP_ROWS = 16
N_DP = 64


def draw_layer_input(key, part):
    key = jax.random.fold_in(key, 3)
    key_noise, key_common, key_spread = jax.random.split(key, 3)
    columns = jnp.arange(D, dtype=jnp.float32) / D
    noise_part = jax.random.normal(key_noise, (TOKENS, D), jnp.float32)
    shared = 0.6
    common = jax.random.normal(key_common, (1, D), jnp.float32)
    spread = jax.random.uniform(key_spread, (1, D), jnp.float32)
    scales = jnp.exp(jnp.log(10.0) * (0.5 * columns + 0.5 * spread))
    return ((noise_part + shared * common) * scales).astype(jnp.bfloat16)


def draw_value_cotangent(key, part):
    key = jax.random.fold_in(key, 5)
    key_noise, key_common, key_rows = jax.random.split(key, 3)
    noise_part = jax.random.normal(key_noise, (TOKENS, KV), jnp.float32)
    shared = 0.6
    reach = jnp.log(10.0)
    common = jax.random.normal(key_common, (1, KV), jnp.float32)
    row_scale = jnp.exp(reach * jax.random.uniform(key_rows, (TOKENS, 1), jnp.float32))
    return ((noise_part + shared * common) * row_scale).astype(jnp.bfloat16)


def draw_owners(key, part):
    key = jax.random.fold_in(key, 11)
    key_order, key_offset = jax.random.split(key)
    shuffled = jax.random.permutation(key_order, N_DP).astype(jnp.int32)
    groups = jnp.arange(N_DP, dtype=jnp.int32)
    offsets = jax.random.randint(key_offset, (N_DP,), 0, CAP).astype(jnp.int32)
    offsets = jnp.where(groups < CAP, groups, offsets)
    buckets = jnp.mod(groups - offsets, N_DP).astype(jnp.int32)
    return shuffled[buckets].astype(jnp.int32)


def plant(values, rng, low, top_value):
    spot = [jax.random.randint(jax.random.fold_in(rng, axis), (), 0, length) for axis, length in enumerate(values.shape)]
    widest = values.shape.index(max(values.shape))
    neighbour = spot[:widest] + [(spot[widest] + 1) % values.shape[widest]] + spot[widest + 1:]
    return values.at[tuple(spot)].set(low).at[tuple(neighbour)].set(top_value)


def block_scale(own_key, extent, cuts, least, largest):
    level = 1.0
    for dim, shards_of in cuts:
        draws = jax.random.uniform(jax.random.fold_in(jax.random.fold_in(own_key, 6), dim), (shards_of,), jnp.float32, least / len(cuts), largest / len(cuts))
        level = level * jnp.repeat(jnp.exp(draws), extent[dim] // shards_of).reshape((-1,) + (1,) * (len(extent) - 1 - dim))
    return level


def length_profile(number_of, total, most, skew):
    portions = [(1 << 20) // math.isqrt(grade ** skew) + 1 for grade in range(2, number_of + 1)]
    surplus, given = total - most - (number_of - 1), [1] * (number_of - 1)
    while surplus > 0:
        movable = [i for i in range(number_of - 1) if given[i] < most]
        whole, left = sum([portions[i] for i in movable]), surplus
        for i in movable:
            extra = min(most - given[i], max(1, left * portions[i] // whole), surplus)
            given[i] = given[i] + extra
            surplus = surplus - extra
    return np.array([most] + given)


def ragged(key, amount, total, most, slope):
    if amount == 2:
        one = jax.random.randint(key, (), max(1, total - most), min(most, total - 1) + 1)
        return jnp.stack([one, total - one])
    lengths = jnp.asarray(length_profile(amount, total, most, slope), jnp.int32)
    couples = (amount - 1) // 2
    giver, taker = lengths[1:1 + 2 * couples:2], lengths[2:2 + 2 * couples:2]
    room = jnp.minimum(giver - 1, most - taker)
    shifted = jax.random.randint(jax.random.fold_in(key, 1), (couples,), 0, 1 << 20) % (room + 1)
    lengths = lengths.at[1:1 + 2 * couples:2].set(giver - shifted).at[2:2 + 2 * couples:2].set(taker + shifted)
    return lengths[jax.random.permutation(jax.random.fold_in(key, 2), amount)]


def centred(key, dims, scale, bound, cuts=(), held_as=jnp.bfloat16):
    gain = block_scale(key, dims, cuts, -0.22, 0.18) if cuts else 1.0
    drawn = jax.random.normal(key, dims, jnp.float32) * scale * gain
    return jnp.minimum(jnp.maximum(drawn, -bound), bound).astype(held_as)


def setup_inputs(seed: int = 0) -> dict:
    streams_of = jax.random.split(jax.random.key(seed), 11)
    return {
        "layer_input": draw_layer_input(jax.random.fold_in(streams_of[10], 71), 0),
        "norm_gain": jnp.clip(1.0 + 0.1 * jax.random.normal(streams_of[1], (D,), jnp.float32), 0.5, 1.5).astype(jnp.bfloat16),
        "value_weight": centred(streams_of[2], (KV, D), D ** -0.5, 0.0625, ((0, 64), (1, 8))),
        "value_cotangent": draw_value_cotangent(jax.random.fold_in(streams_of[10], 71), 0),
        "doc_ids": jnp.searchsorted(jnp.cumsum(ragged(streams_of[4], 2 * N_DP, TOKENS, TOK_DEV, 2)), jnp.arange(TOKENS), side="right").astype(jnp.int32),
        "owners": draw_owners(jax.random.fold_in(streams_of[10], 71), 0),
        "noise_seeds": plant(jax.random.randint(streams_of[6], (N_DP,), 0, 2**30), jax.random.fold_in(streams_of[6], 1), 0, (2**30) - 1).astype(jnp.int32),
        "master": centred(streams_of[7], (CAP * KV, D), 0.02, 0.12, ((0, 64), (1, 8)), jnp.float32),
        "moment_one": centred(streams_of[8], (CAP * KV, D), 1.0, 6.0, ((0, 64), (1, 8)), jnp.float32),
        "moment_two": jnp.clip(jnp.exp(math.log(8.0) - 2.7725887 * jax.random.uniform(streams_of[9], (CAP * KV, D), jnp.float32) ** block_scale(streams_of[9], (CAP * KV, D), ((0, 64), (1, 8)), -0.2, 0.2)), 0.5, 8.0),
    }


EPS_NORM = 1e-06
CLIP_NORM = 128.0
NOISE_MULT = 0.01
LEARN_RATE = 0.001
BETA_ONE = 0.9
BETA_TWO = 0.999
ADAM_STEP = 100
ADAM_EPS = 1e-08

def mix_bits(bits_in):
    bits_in = jnp.bitwise_xor(bits_in, lax.shift_right_logical(bits_in, jnp.int32(16)))
    bits_in = bits_in * jnp.int32(2146121005)
    bits_in = jnp.bitwise_xor(bits_in, lax.shift_right_logical(bits_in, jnp.int32(15)))
    bits_in = bits_in * jnp.int32(-2073254261)
    bits_in = jnp.bitwise_xor(bits_in, lax.shift_right_logical(bits_in, jnp.int32(16)))
    return bits_in

def unit_draw(seed_value, position):
    hashed = mix_bits(mix_bits(jnp.bitwise_xor(position, seed_value)) + seed_value)
    return (lax.shift_right_logical(hashed, jnp.int32(8)).astype(jnp.float32) + 0.5) * (1.0 / 16777216.0)

def gauss_noise(seed_value, position):
    draw_one = unit_draw(seed_value, 2 * position)
    draw_two = unit_draw(seed_value, 2 * position + 1)
    return jnp.sqrt(-2.0 * jnp.log(draw_one)) * jnp.cos(6.283185307179586 * draw_two)

def reference(layer_input, norm_gain, value_weight, value_cotangent, doc_ids, owners, noise_seeds, master, moment_one, moment_two):
    inputs = layer_input.astype(jnp.float32)
    gain_row = norm_gain.astype(jnp.float32)
    inv_rms = lax.rsqrt(lax.optimization_barrier(jnp.mean(inputs * inputs, axis=1, keepdims=True)) + EPS_NORM)
    normed = (inputs * inv_rms * gain_row).astype(jnp.bfloat16)
    dnormed = jnp.dot(value_cotangent, value_weight, preferred_element_type=jnp.float32)
    weighted = gain_row * dnormed
    inner_sum = lax.optimization_barrier(jnp.sum(weighted * inputs, axis=1, keepdims=True)) / D
    input_grad = (inv_rms * weighted - inputs * inv_rms * inv_rms * inv_rms * inner_sum).astype(jnp.bfloat16)
    normed_seqs = normed.reshape(N_DP, TOK_DEV, D)
    cot_seqs = value_cotangent.reshape(N_DP, TOK_DEV, KV)
    doc_seqs = doc_ids.reshape(N_DP, TOK_DEV)

    def seq_scale(seq_block):
        normed_block, cot_block, doc_block = seq_block
        gram_features = jnp.dot(normed_block, normed_block.T, preferred_element_type=jnp.float32)
        gram_values = jnp.dot(cot_block, cot_block.T, preferred_element_type=jnp.float32)
        same_doc = (doc_block[:, None] == doc_block[None, :]).astype(jnp.float32)
        row_sums = lax.optimization_barrier(jnp.sum(same_doc * gram_features * gram_values, axis=1))
        squared = jnp.dot(same_doc, row_sums, precision=lax.Precision.HIGHEST)
        return CLIP_NORM / (jnp.sqrt(squared) + 0.01)
    scales = lax.map(seq_scale, (normed_seqs, cot_seqs, doc_seqs)).reshape(TOKENS, 1)
    clipped = (value_cotangent.astype(jnp.float32) * scales).astype(jnp.bfloat16)
    weight_grad = lax.dot_general(clipped, normed, (((0,), (0,)), ((), ())), preferred_element_type=jnp.float32)
    row_idx = jnp.arange(KV, dtype=jnp.int32)
    col_idx = jnp.arange(D, dtype=jnp.int32)
    positions = (row_idx % GROUP_ROWS)[:, None] * D + col_idx[None, :]
    row_seeds = noise_seeds[row_idx // GROUP_ROWS][:, None]
    noisy = weight_grad + NOISE_MULT * CLIP_NORM * gauss_noise(row_seeds, positions)
    group_ids = jnp.arange(N_DP, dtype=jnp.int32)
    earlier = group_ids[:, None] > group_ids[None, :]
    same_owner = owners[:, None] == owners[None, :]
    slot_rank = lax.optimization_barrier(jnp.sum((earlier & same_owner).astype(jnp.int32), axis=1))
    targets = (owners * CAP + slot_rank).astype(jnp.int32)
    noisy_groups = noisy.reshape(N_DP, GROUP_ROWS, D)
    master_slots = master.reshape(N_DP * CAP, GROUP_ROWS, D)
    first_slots = moment_one.reshape(N_DP * CAP, GROUP_ROWS, D)
    second_slots = moment_two.reshape(N_DP * CAP, GROUP_ROWS, D)
    first_new = BETA_ONE * first_slots[targets] + (1.0 - BETA_ONE) * noisy_groups
    second_new = BETA_TWO * second_slots[targets] + (1.0 - BETA_TWO) * noisy_groups * noisy_groups
    update = first_new / (1.0 - BETA_ONE ** ADAM_STEP) / (jnp.sqrt(second_new / (1.0 - BETA_TWO ** ADAM_STEP)) + ADAM_EPS)
    master_new = master_slots[targets] - LEARN_RATE * update
    new_master = master_slots.at[targets].set(master_new).reshape(CAP * KV, D)
    new_moment_one = first_slots.at[targets].set(first_new).reshape(CAP * KV, D)
    new_moment_two = second_slots.at[targets].set(second_new).reshape(CAP * KV, D)
    return (input_grad, new_master, new_moment_one, new_moment_two)
```

```python
import jax
import jax.numpy as jnp
from jax import lax
from jax.sharding import Mesh
from jax.sharding import PartitionSpec as P

EPS_NORM = 1e-06
CLIP_NORM = 128.0
NOISE_MULT = 0.01
LEARN_RATE = 0.001
BETA_ONE = 0.9
BETA_TWO = 0.999
ADAM_STEP = 100
ADAM_EPS = 1e-08

DP_SPLIT = (2, 4, 4, 2)
DP_AXES = ("zh", "y", "x", "core")
PLANE = ("y", "x")
BF16 = jnp.bfloat16
F32 = jnp.float32


def mix_bits(bits_in):
    bits_in = jnp.bitwise_xor(bits_in, lax.shift_right_logical(bits_in, jnp.int32(16)))
    bits_in = bits_in * jnp.int32(2146121005)
    bits_in = jnp.bitwise_xor(bits_in, lax.shift_right_logical(bits_in, jnp.int32(15)))
    bits_in = bits_in * jnp.int32(-2073254261)
    bits_in = jnp.bitwise_xor(bits_in, lax.shift_right_logical(bits_in, jnp.int32(16)))
    return bits_in


def unit_draw(seed_value, position):
    hashed = mix_bits(mix_bits(jnp.bitwise_xor(position, seed_value)) + seed_value)
    return (lax.shift_right_logical(hashed, jnp.int32(8)).astype(F32) + 0.5) * (1.0 / 16777216.0)


def gauss_noise(seed_value, position):
    draw_one = unit_draw(seed_value, 2 * position)
    draw_two = unit_draw(seed_value, 2 * position + 1)
    return jnp.sqrt(-2.0 * jnp.log(draw_one)) * jnp.cos(6.283185307179586 * draw_two)


def body(
    layer_input,
    norm_gain,
    value_weight,
    value_cotangent,
    doc_ids,
    owners,
    noise_seeds,
    master,
    moment_one,
    moment_two,
):
    tokens, part_width = layer_input.shape
    cot_part = value_cotangent.shape[1]
    n_mp = lax.axis_size("mp")
    n_zh, n_core = lax.axis_size("zh"), lax.axis_size("core")
    n_yx = lax.axis_size("y") * lax.axis_size("x")
    full_width = part_width * n_mp
    group_rows = value_weight.shape[0]
    n_groups = owners.shape[0]
    value_width = n_groups * group_rows
    slots = master.shape[0] // group_rows
    half = part_width // n_core
    my_core = lax.axis_index("core")
    my_column = lax.axis_index("mp")
    my_zh = lax.axis_index("zh")
    my_yx = lax.axis_index(PLANE)
    my_group = lax.axis_index(DP_AXES)
    swap = [(0, 1), (1, 0)]

    inputs = layer_input.astype(F32)
    gain_row = norm_gain.astype(F32)

    squares_part = jnp.sum(inputs * inputs, axis=1)
    term_one = squares_part.astype(BF16)
    rest = squares_part - term_one.astype(F32)
    term_two = rest.astype(BF16)
    term_three = (rest - term_two.astype(F32)).astype(BF16)
    terms = jnp.concatenate([term_one, term_two, term_three]).reshape(-1, cot_part)
    n_terms = terms.shape[0]
    packet = jnp.concatenate([value_cotangent, terms], axis=0)
    packets = lax.all_to_all(
        jnp.broadcast_to(packet[None], (n_mp,) + packet.shape), "mp", 0, 0
    )
    full_cot = packets[:, :tokens].transpose(1, 0, 2).reshape(tokens, value_width)
    squares = jnp.sum(
        packets[:, tokens : tokens + n_terms].astype(F32).reshape(n_mp * 3, tokens), axis=0
    )
    inv_rms = lax.rsqrt(squares / full_width + EPS_NORM)

    weight_far = lax.ppermute(value_weight, "zh", swap)
    low = jnp.where(my_zh == 0, value_weight, weight_far)
    high = jnp.where(my_zh == 0, weight_far, value_weight)
    weight_pair = jnp.stack([low, high])
    weight_own = lax.all_to_all(
        jnp.broadcast_to(weight_pair[None], (n_yx,) + weight_pair.shape), PLANE, 0, 0
    )
    weight_other = lax.ppermute(weight_own, "core", swap)
    even = jnp.where(my_core == 0, weight_own, weight_other)
    odd = jnp.where(my_core == 0, weight_other, weight_own)
    full_weight = jnp.stack([even, odd]).transpose(2, 1, 0, 3, 4).reshape(value_width, part_width)

    gained = (inputs * gain_row).astype(BF16)
    gram_features = jnp.dot(gained, gained.T, preferred_element_type=F32)
    gram_values = jnp.dot(full_cot, full_cot.T, preferred_element_type=F32)
    same_doc = doc_ids[:, None] == doc_ids[None, :]
    row_part = inv_rms * jnp.sum(
        jnp.where(same_doc, gram_features * gram_values * inv_rms[None, :], 0.0), axis=1
    )
    squared_part = jnp.sum(jnp.where(same_doc, row_part[None, :], 0.0), axis=1)

    dnormed = jnp.dot(full_cot, full_weight, preferred_element_type=F32)
    weighted = gain_row * dnormed
    inner_part = jnp.sum(weighted * inputs, axis=1)

    sums_packet = jnp.stack([squared_part, inner_part]).reshape(-1, 128)
    sums_all = lax.all_to_all(
        jnp.broadcast_to(sums_packet[None], (n_core * n_mp,) + sums_packet.shape),
        ("core", "mp"),
        0,
        0,
    )
    sums_all = jnp.sum(sums_all.reshape(n_core, n_mp, 2, tokens), axis=1)
    sums_own = jnp.where(my_core == 0, sums_all[0], sums_all[1])
    sums_other = jnp.where(my_core == 0, sums_all[1], sums_all[0])
    scales_own = CLIP_NORM / (jnp.sqrt(sums_own[0]) + 0.01)
    scales_other = CLIP_NORM / (jnp.sqrt(sums_other[0]) + 0.01)
    inv_col = inv_rms[:, None]
    input_grad = (
        inv_col * weighted
        - inputs * inv_col * inv_col * inv_col * (sums_own[1] / full_width)[:, None]
    ).astype(BF16)

    normed = (inputs * inv_col * gain_row).astype(BF16)
    normed_other = lax.ppermute(
        lax.dynamic_slice(normed, (0, (1 - my_core) * half), (tokens, half)), "core", swap
    )
    normed_own = lax.dynamic_slice(normed, (0, my_core * half), (tokens, half))
    k_pos = jnp.arange(value_width, dtype=jnp.int32)
    target = (k_pos % group_rows) * n_groups + k_pos // group_rows
    reorder = (target[:, None] == k_pos[None, :]).astype(BF16)
    cot_own = jnp.dot(full_cot, reorder, preferred_element_type=F32).astype(BF16)
    cot_other = lax.ppermute(cot_own, "core", swap)
    clipped_own = (cot_own.astype(F32) * scales_own[:, None]).astype(BF16)
    clipped_other = (cot_other.astype(F32) * scales_other[:, None]).astype(BF16)
    grad_chip = lax.dot_general(
        clipped_own, normed_own, (((0,), (0,)), ((), ())), preferred_element_type=F32
    ) + lax.dot_general(
        clipped_other, normed_other, (((0,), (0,)), ((), ())), preferred_element_type=F32
    )
    grad_rows = grad_chip.astype(BF16).reshape(group_rows, n_groups, half)
    grad_rows = lax.all_to_all(grad_rows, PLANE, 0, 0)
    grad_plane = jnp.sum(grad_rows.astype(F32), axis=0)
    grad_far = lax.ppermute(grad_plane, "zh", swap)
    col_pos = my_column * part_width + my_core * half + jnp.arange(half, dtype=jnp.int32)[None, :]
    noise = gauss_noise(noise_seeds[:, None], my_yx * full_width + col_pos)
    noisy = grad_plane + grad_far + NOISE_MULT * CLIP_NORM * noise

    group_ids = jnp.arange(n_groups, dtype=jnp.int32)
    earlier = group_ids[:, None] > group_ids[None, :]
    same_owner = owners[:, None] == owners[None, :]
    slot_rank = jnp.sum((earlier & same_owner).astype(jnp.int32), axis=1)
    n_dest = n_groups // n_zh
    place = (owners - my_zh * n_dest) * slots + slot_rank
    places = jnp.arange(n_dest * slots, dtype=jnp.int32)
    sends = (places[:, None] == place[None, :]).astype(F32)
    outgoing = jnp.dot(sends, noisy, precision=lax.Precision.HIGHEST).reshape(n_dest, slots, half)
    arrived = lax.all_to_all(outgoing, PLANE + ("core",), 0, 0)
    gathered = (
        arrived.reshape(n_yx, n_core, slots, half)
        .transpose(2, 0, 1, 3)
        .reshape(slots * group_rows, part_width)
    )
    slot_ids = jnp.arange(slots, dtype=jnp.int32)
    filled = jnp.any(
        (owners[None, :] == my_group) & (slot_rank[None, :] == slot_ids[:, None]), axis=1
    )
    keep_mask = jnp.repeat(filled, group_rows)[:, None]
    first_new = BETA_ONE * moment_one + (1.0 - BETA_ONE) * gathered
    second_new = BETA_TWO * moment_two + (1.0 - BETA_TWO) * gathered * gathered
    update = (
        first_new
        / (1.0 - BETA_ONE**ADAM_STEP)
        / (jnp.sqrt(second_new / (1.0 - BETA_TWO**ADAM_STEP)) + ADAM_EPS)
    )
    new_master = jnp.where(keep_mask, master - LEARN_RATE * update, master)
    new_moment_one = jnp.where(keep_mask, first_new, moment_one)
    new_moment_two = jnp.where(keep_mask, second_new, moment_two)
    return (input_grad, new_master, new_moment_one, new_moment_two)


def solution(mesh, dp_split=DP_SPLIT):
    fine = Mesh(mesh.devices.reshape(dp_split + (mesh.shape["mp"],)), DP_AXES + ("mp",))
    rows, both = P(DP_AXES), P(DP_AXES, "mp")
    in_specs = (both, P("mp"), both, both, rows, P(), P(), both, both, both)
    out_specs = (both, both, both, both)
    return jax.shard_map(body, mesh=fine, in_specs=in_specs, out_specs=out_specs, check_vma=False)
```

```python
import jax
import jax.numpy as jnp
from jax import lax
from jax.sharding import Mesh
from jax.sharding import PartitionSpec as P

EPS_NORM = 1e-06
CLIP_NORM = 128.0
NOISE_MULT = 0.01
LEARN_RATE = 0.001
BETA_ONE = 0.9
BETA_TWO = 0.999
ADAM_STEP = 100
ADAM_EPS = 1e-08

DP_SPLIT = (2, 4, 4, 2)
DP_AXES = ("zh", "y", "x", "core")
PLANE = ("y", "x")
BF16 = jnp.bfloat16
F32 = jnp.float32


def mix_bits(bits_in):
    bits_in = jnp.bitwise_xor(bits_in, lax.shift_right_logical(bits_in, jnp.int32(16)))
    bits_in = bits_in * jnp.int32(2146121005)
    bits_in = jnp.bitwise_xor(bits_in, lax.shift_right_logical(bits_in, jnp.int32(15)))
    bits_in = bits_in * jnp.int32(-2073254261)
    bits_in = jnp.bitwise_xor(bits_in, lax.shift_right_logical(bits_in, jnp.int32(16)))
    return bits_in


def unit_draw(seed_value, position):
    hashed = mix_bits(mix_bits(jnp.bitwise_xor(position, seed_value)) + seed_value)
    return (lax.shift_right_logical(hashed, jnp.int32(8)).astype(F32) + 0.5) * (1.0 / 16777216.0)


def gauss_noise(seed_value, position):
    draw_one = unit_draw(seed_value, 2 * position)
    draw_two = unit_draw(seed_value, 2 * position + 1)
    return jnp.sqrt(-2.0 * jnp.log(draw_one)) * jnp.cos(6.283185307179586 * draw_two)


def body(
    layer_input,
    norm_gain,
    value_weight,
    value_cotangent,
    doc_ids,
    owners,
    noise_seeds,
    master,
    moment_one,
    moment_two,
):
    tokens, part_width = layer_input.shape
    cot_part = value_cotangent.shape[1]
    n_mp = lax.axis_size("mp")
    n_zh, n_core = lax.axis_size("zh"), lax.axis_size("core")
    n_yx = lax.axis_size("y") * lax.axis_size("x")
    full_width = part_width * n_mp
    group_rows = value_weight.shape[0]
    n_groups = owners.shape[0]
    value_width = n_groups * group_rows
    slots = master.shape[0] // group_rows
    half = part_width // n_core
    my_core = lax.axis_index("core")
    my_column = lax.axis_index("mp")
    my_zh = lax.axis_index("zh")
    my_yx = lax.axis_index(PLANE)
    my_group = lax.axis_index(DP_AXES)
    swap = [(0, 1), (1, 0)]

    inputs = layer_input.astype(F32)
    gain_row = norm_gain.astype(F32)

    squares_part = jnp.sum(inputs * inputs, axis=1)
    term_one = lax.reduce_precision(squares_part, 8, 7)
    rest = squares_part - term_one
    term_two = lax.reduce_precision(rest, 8, 7)
    terms = jnp.concatenate([term_one, term_two, rest - term_two]).astype(BF16)
    terms = terms.reshape(-1, cot_part)
    n_terms = terms.shape[0]
    packets = jnp.concatenate([value_cotangent, terms], axis=0)
    held = packets.shape[0]
    packets = packets[None]
    bit = n_mp // 2
    level = 0
    while bit:
        far = lax.ppermute(packets, "mp", [(i, i ^ bit) for i in range(n_mp)])
        first = (my_column & bit) == 0
        packets = jnp.stack(
            [jnp.where(first, packets, far), jnp.where(first, far, packets)], axis=1
        ).reshape(2 << level, held, cot_part)
        bit //= 2
        level += 1
    full_cot = packets[:, :tokens].transpose(1, 0, 2).reshape(tokens, value_width)
    squares = jnp.sum(packets[:, tokens:].astype(F32).reshape(n_mp * 3, tokens), axis=0)
    inv_rms = lax.rsqrt(squares / full_width + EPS_NORM)

    weight_far = lax.ppermute(value_weight, "zh", swap)
    low = jnp.where(my_zh == 0, value_weight, weight_far)
    high = jnp.where(my_zh == 0, weight_far, value_weight)
    weight_pair = jnp.stack([low, high])
    weight_own = lax.all_to_all(
        jnp.broadcast_to(weight_pair[None], (n_yx,) + weight_pair.shape), PLANE, 0, 0
    )
    weight_other = lax.ppermute(weight_own, "core", swap)
    even = jnp.where(my_core == 0, weight_own, weight_other)
    odd = jnp.where(my_core == 0, weight_other, weight_own)
    full_weight = jnp.stack([even, odd]).transpose(2, 1, 0, 3, 4).reshape(value_width, part_width)

    gained = (inputs * gain_row).astype(BF16)
    gram_features = jnp.dot(gained, gained.T, preferred_element_type=F32)
    gram_values = jnp.dot(full_cot, full_cot.T, preferred_element_type=F32)
    same_doc = doc_ids[:, None] == doc_ids[None, :]
    row_part = inv_rms * jnp.sum(
        jnp.where(same_doc, gram_features * gram_values * inv_rms[None, :], 0.0), axis=1
    )
    squared_part = jnp.sum(jnp.where(same_doc, row_part[None, :], 0.0), axis=1)

    dnormed = jnp.dot(full_cot, full_weight, preferred_element_type=F32)
    weighted = gain_row * dnormed
    inner_part = jnp.sum(weighted * inputs, axis=1)

    sums_packet = jnp.stack([squared_part, inner_part]).reshape(-1, 128)
    sums_all = lax.all_to_all(
        jnp.broadcast_to(sums_packet[None], (n_core * n_mp,) + sums_packet.shape),
        ("core", "mp"),
        0,
        0,
    )
    sums_all = jnp.sum(sums_all.reshape(n_core, n_mp, 2, tokens), axis=1)
    sums_own = jnp.where(my_core == 0, sums_all[0], sums_all[1])
    sums_other = jnp.where(my_core == 0, sums_all[1], sums_all[0])
    scales_own = CLIP_NORM / (jnp.sqrt(sums_own[0]) + 0.01)
    scales_other = CLIP_NORM / (jnp.sqrt(sums_other[0]) + 0.01)

    inv_col = inv_rms[:, None]
    normed = (inputs * inv_col * gain_row).astype(BF16)
    normed_other = lax.ppermute(
        lax.dynamic_slice(normed, (0, (1 - my_core) * half), (tokens, half)), "core", swap
    )
    normed_own = lax.dynamic_slice(normed, (0, my_core * half), (tokens, half))
    k_pos = jnp.arange(value_width, dtype=jnp.int32)
    target = (k_pos % group_rows) * n_groups + k_pos // group_rows
    reorder = (target[None, :] == k_pos[:, None]).astype(BF16)
    cot_own = lax.dot_general(
        reorder, full_cot, (((1,), (1,)), ((), ())), preferred_element_type=F32
    ).astype(BF16)
    cot_other = lax.ppermute(cot_own, "core", swap)
    clipped = jnp.concatenate(
        [
            (cot_own.astype(F32) * scales_own[None, :]).astype(BF16),
            (cot_other.astype(F32) * scales_other[None, :]).astype(BF16),
        ],
        axis=1,
    )
    normed_both = jnp.concatenate([normed_own, normed_other], axis=0)
    grad_chip = jnp.dot(clipped, normed_both, preferred_element_type=F32)
    grad_rows = grad_chip.astype(BF16).reshape(group_rows, n_groups, half)
    grad_rows, inner_sum = lax.optimization_barrier((grad_rows, sums_own[1]))
    input_grad = (
        inv_col * weighted
        - inputs * inv_col * inv_col * inv_col * (inner_sum / full_width)[:, None]
    ).astype(BF16)

    grad_rows = lax.all_to_all(grad_rows, PLANE, 0, 0)
    grad_plane = jnp.sum(grad_rows.astype(F32), axis=0)
    grad_far = lax.ppermute(grad_plane, "zh", swap)
    col_pos = my_column * part_width + my_core * half + jnp.arange(half, dtype=jnp.int32)[None, :]
    noise = gauss_noise(noise_seeds[:, None], my_yx * full_width + col_pos)
    noisy = grad_plane + grad_far + NOISE_MULT * CLIP_NORM * noise

    group_ids = jnp.arange(n_groups, dtype=jnp.int32)
    earlier = group_ids[:, None] > group_ids[None, :]
    same_owner = owners[:, None] == owners[None, :]
    slot_rank = jnp.sum((earlier & same_owner).astype(jnp.int32), axis=1)
    n_dest = n_groups // n_zh
    place = (owners - my_zh * n_dest) * slots + slot_rank
    places = jnp.arange(n_dest * slots, dtype=jnp.int32)
    sends = (places[:, None] == place[None, :]).astype(F32)
    outgoing = jnp.dot(sends, noisy, precision=lax.Precision.HIGHEST).reshape(n_dest, slots, half)
    arrived = lax.all_to_all(outgoing, PLANE + ("core",), 0, 0)
    gathered = (
        arrived.reshape(n_yx, n_core, slots, half)
        .transpose(2, 0, 1, 3)
        .reshape(slots * group_rows, part_width)
    )
    slot_ids = jnp.arange(slots, dtype=jnp.int32)
    filled = jnp.any(
        (owners[None, :] == my_group) & (slot_rank[None, :] == slot_ids[:, None]), axis=1
    )
    keep_mask = jnp.repeat(filled, group_rows)[:, None]
    first_new = BETA_ONE * moment_one + (1.0 - BETA_ONE) * gathered
    second_new = BETA_TWO * moment_two + (1.0 - BETA_TWO) * gathered * gathered
    update = (
        first_new
        / (1.0 - BETA_ONE**ADAM_STEP)
        / (jnp.sqrt(second_new / (1.0 - BETA_TWO**ADAM_STEP)) + ADAM_EPS)
    )
    new_master = jnp.where(keep_mask, master - LEARN_RATE * update, master)
    new_moment_one = jnp.where(keep_mask, first_new, moment_one)
    new_moment_two = jnp.where(keep_mask, second_new, moment_two)
    return (input_grad, new_master, new_moment_one, new_moment_two)


def solution(mesh, dp_split=DP_SPLIT):
    fine = Mesh(mesh.devices.reshape(dp_split + (mesh.shape["mp"],)), DP_AXES + ("mp",))
    rows, both = P(DP_AXES), P(DP_AXES, "mp")
    in_specs = (both, P("mp"), both, both, rows, P(), P(), both, both, both)
    out_specs = (both, both, both, both)
    return jax.shard_map(body, mesh=fine, in_specs=in_specs, out_specs=out_specs, check_vma=False)
```

```python
import jax
import jax.numpy as jnp
from jax import lax
from jax.sharding import Mesh
from jax.sharding import PartitionSpec as P

EPS_NORM = 1e-06
CLIP_NORM = 128.0
NOISE_MULT = 0.01
LEARN_RATE = 0.001
BETA_ONE = 0.9
BETA_TWO = 0.999
ADAM_STEP = 100
ADAM_EPS = 1e-08

DP_SPLIT = (2, 4, 4, 2)
DP_AXES = ("zh", "y", "x", "core")
PLANE = ("y", "x")
BF16 = jnp.bfloat16
F32 = jnp.float32


def mix_bits(bits_in):
    bits_in = jnp.bitwise_xor(bits_in, lax.shift_right_logical(bits_in, jnp.int32(16)))
    bits_in = bits_in * jnp.int32(2146121005)
    bits_in = jnp.bitwise_xor(bits_in, lax.shift_right_logical(bits_in, jnp.int32(15)))
    bits_in = bits_in * jnp.int32(-2073254261)
    bits_in = jnp.bitwise_xor(bits_in, lax.shift_right_logical(bits_in, jnp.int32(16)))
    return bits_in


def unit_draw(seed_value, position):
    hashed = mix_bits(mix_bits(jnp.bitwise_xor(position, seed_value)) + seed_value)
    return (lax.shift_right_logical(hashed, jnp.int32(8)).astype(F32) + 0.5) * (1.0 / 16777216.0)


def gauss_noise(seed_value, position):
    draw_one = unit_draw(seed_value, 2 * position)
    draw_two = unit_draw(seed_value, 2 * position + 1)
    return jnp.sqrt(-2.0 * jnp.log(draw_one)) * jnp.cos(6.283185307179586 * draw_two)


def body(
    layer_input,
    norm_gain,
    value_weight,
    value_cotangent,
    doc_ids,
    owners,
    noise_seeds,
    master,
    moment_one,
    moment_two,
):
    tokens, part_width = layer_input.shape
    cot_part = value_cotangent.shape[1]
    n_mp = lax.axis_size("mp")
    n_zh, n_core = lax.axis_size("zh"), lax.axis_size("core")
    n_yx = lax.axis_size("y") * lax.axis_size("x")
    full_width = part_width * n_mp
    group_rows = value_weight.shape[0]
    n_groups = owners.shape[0]
    value_width = n_groups * group_rows
    slots = master.shape[0] // group_rows
    half = part_width // n_core
    my_core = lax.axis_index("core")
    my_column = lax.axis_index("mp")
    my_zh = lax.axis_index("zh")
    my_yx = lax.axis_index(PLANE)
    my_group = lax.axis_index(DP_AXES)
    swap = [(0, 1), (1, 0)]

    inputs = layer_input.astype(F32)
    gain_row = norm_gain.astype(F32)

    squares_part = jnp.sum(inputs * inputs, axis=1)
    term_one = lax.reduce_precision(squares_part, 8, 7)
    rest = squares_part - term_one
    term_two = lax.reduce_precision(rest, 8, 7)
    terms = jnp.concatenate([term_one, term_two, rest - term_two]).astype(BF16)
    terms = terms.reshape(-1, cot_part)
    n_terms = terms.shape[0]
    packets = jnp.concatenate([value_cotangent, terms], axis=0)
    held = packets.shape[0]
    packets = packets[None]
    weight_far = lax.ppermute(value_weight, "zh", swap)
    bit = n_mp // 2
    level = 0
    while bit:
        far = lax.ppermute(packets, "mp", [(i, i ^ bit) for i in range(n_mp)])
        if level == 0:
            far, weight_far = lax.optimization_barrier((far, weight_far))
        first = (my_column & bit) == 0
        packets = jnp.stack(
            [jnp.where(first, packets, far), jnp.where(first, far, packets)], axis=1
        ).reshape(2 << level, held, cot_part)
        bit //= 2
        level += 1
    full_cot = packets[:, :tokens].transpose(1, 0, 2).reshape(tokens, value_width)
    squares = jnp.sum(packets[:, tokens:].astype(F32).reshape(n_mp * 3, tokens), axis=0)
    inv_rms = lax.rsqrt(squares / full_width + EPS_NORM)

    low = jnp.where(my_zh == 0, value_weight, weight_far)
    high = jnp.where(my_zh == 0, weight_far, value_weight)
    weight_pair = jnp.stack([low, high])
    weight_own = lax.all_to_all(
        jnp.broadcast_to(weight_pair[None], (n_yx,) + weight_pair.shape), PLANE, 0, 0
    )
    weight_other = lax.ppermute(weight_own, "core", swap)
    even = jnp.where(my_core == 0, weight_own, weight_other)
    odd = jnp.where(my_core == 0, weight_other, weight_own)
    full_weight = jnp.stack([even, odd]).transpose(2, 1, 0, 3, 4).reshape(value_width, part_width)

    gained = (inputs * gain_row).astype(BF16)
    gram_features = jnp.dot(gained, gained.T, preferred_element_type=F32)
    gram_values = jnp.dot(full_cot, full_cot.T, preferred_element_type=F32)
    same_doc = doc_ids[:, None] == doc_ids[None, :]
    row_part = inv_rms * jnp.sum(
        jnp.where(same_doc, gram_features * gram_values * inv_rms[None, :], 0.0), axis=1
    )
    squared_part = jnp.sum(jnp.where(same_doc, row_part[None, :], 0.0), axis=1)

    dnormed = jnp.dot(full_cot, full_weight, preferred_element_type=F32)
    weighted = gain_row * dnormed
    inner_part = jnp.sum(weighted * inputs, axis=1)

    sums_packet = jnp.stack([squared_part, inner_part]).reshape(-1, 128)
    sums_all = lax.all_to_all(
        jnp.broadcast_to(sums_packet[None], (n_core * n_mp,) + sums_packet.shape),
        ("core", "mp"),
        0,
        0,
    )
    inv_col = inv_rms[:, None]
    normed = (inputs * inv_col * gain_row).astype(BF16)
    normed_other = lax.ppermute(
        lax.dynamic_slice(normed, (0, (1 - my_core) * half), (tokens, half)), "core", swap
    )
    normed_own = lax.dynamic_slice(normed, (0, my_core * half), (tokens, half))
    k_pos = jnp.arange(value_width, dtype=jnp.int32)
    target = (k_pos % group_rows) * n_groups + k_pos // group_rows
    reorder = (target[None, :] == k_pos[:, None]).astype(BF16)
    cot_own = lax.dot_general(
        reorder, full_cot, (((1,), (1,)), ((), ())), preferred_element_type=F32
    ).astype(BF16)
    cot_other = lax.ppermute(cot_own, "core", swap)
    sums_all, cot_other, normed_other = lax.optimization_barrier(
        (sums_all, cot_other, normed_other)
    )
    sums_all = jnp.sum(sums_all.reshape(n_core, n_mp, 2, tokens), axis=1)
    sums_own = jnp.where(my_core == 0, sums_all[0], sums_all[1])
    sums_other = jnp.where(my_core == 0, sums_all[1], sums_all[0])
    scales_own = CLIP_NORM / (jnp.sqrt(sums_own[0]) + 0.01)
    scales_other = CLIP_NORM / (jnp.sqrt(sums_other[0]) + 0.01)

    clipped = jnp.concatenate(
        [
            (cot_own.astype(F32) * scales_own[None, :]).astype(BF16),
            (cot_other.astype(F32) * scales_other[None, :]).astype(BF16),
        ],
        axis=1,
    )
    normed_both = jnp.concatenate([normed_own, normed_other], axis=0)
    grad_chip = jnp.dot(clipped, normed_both, preferred_element_type=F32)
    grad_rows = grad_chip.astype(BF16).reshape(group_rows, n_groups, half)
    grad_rows, inner_sum = lax.optimization_barrier((grad_rows, sums_own[1]))
    input_grad = (
        inv_col * weighted
        - inputs * inv_col * inv_col * inv_col * (inner_sum / full_width)[:, None]
    ).astype(BF16)

    grad_rows = lax.all_to_all(grad_rows, PLANE, 0, 0)
    grad_plane = jnp.sum(grad_rows.astype(F32), axis=0)
    grad_far = lax.ppermute(grad_plane, "zh", swap)
    col_pos = my_column * part_width + my_core * half + jnp.arange(half, dtype=jnp.int32)[None, :]
    noise = gauss_noise(noise_seeds[:, None], my_yx * full_width + col_pos)
    noisy = grad_plane + grad_far + NOISE_MULT * CLIP_NORM * noise

    group_ids = jnp.arange(n_groups, dtype=jnp.int32)
    earlier = group_ids[:, None] > group_ids[None, :]
    same_owner = owners[:, None] == owners[None, :]
    slot_rank = jnp.sum((earlier & same_owner).astype(jnp.int32), axis=1)
    n_dest = n_groups // n_zh
    place = (owners - my_zh * n_dest) * slots + slot_rank
    places = jnp.arange(n_dest * slots, dtype=jnp.int32)
    sends = (places[:, None] == place[None, :]).astype(F32)
    outgoing = jnp.dot(sends, noisy, precision=lax.Precision.HIGHEST).reshape(n_dest, slots, half)
    arrived = lax.all_to_all(outgoing, PLANE + ("core",), 0, 0)
    gathered = (
        arrived.reshape(n_yx, n_core, slots, half)
        .transpose(2, 0, 1, 3)
        .reshape(slots * group_rows, part_width)
    )
    slot_ids = jnp.arange(slots, dtype=jnp.int32)
    filled = jnp.any(
        (owners[None, :] == my_group) & (slot_rank[None, :] == slot_ids[:, None]), axis=1
    )
    keep_mask = jnp.repeat(filled, group_rows)[:, None]
    first_new = BETA_ONE * moment_one + (1.0 - BETA_ONE) * gathered
    second_new = BETA_TWO * moment_two + (1.0 - BETA_TWO) * gathered * gathered
    update = (
        first_new
        / (1.0 - BETA_ONE**ADAM_STEP)
        / (jnp.sqrt(second_new / (1.0 - BETA_TWO**ADAM_STEP)) + ADAM_EPS)
    )
    new_master = jnp.where(keep_mask, master - LEARN_RATE * update, master)
    new_moment_one = jnp.where(keep_mask, first_new, moment_one)
    new_moment_two = jnp.where(keep_mask, second_new, moment_two)
    return (input_grad, new_master, new_moment_one, new_moment_two)


def solution(mesh, dp_split=DP_SPLIT):
    fine = Mesh(mesh.devices.reshape(dp_split + (mesh.shape["mp"],)), DP_AXES + ("mp",))
    rows, both = P(DP_AXES), P(DP_AXES, "mp")
    in_specs = (both, P("mp"), both, both, rows, P(), P(), both, both, both)
    out_specs = (both, both, both, both)
    return jax.shard_map(body, mesh=fine, in_specs=in_specs, out_specs=out_specs, check_vma=False)
```

```python
import functools

import jax
import jax.numpy as jnp
from jax import lax
from jax.experimental import pallas as pl
from jax.experimental.pallas import tpu as pltpu
from jax.sharding import Mesh
from jax.sharding import PartitionSpec as P

EPS_NORM = 1e-06
CLIP_NORM = 128.0
NOISE_MULT = 0.01
LEARN_RATE = 0.001
BETA_ONE = 0.9
BETA_TWO = 0.999
ADAM_STEP = 100
ADAM_EPS = 1e-08

DP_SPLIT = (2, 4, 4, 2)
DP_AXES = ("zh", "y", "x", "core")
PLANE = ("y", "x")
BF16 = jnp.bfloat16
F32 = jnp.float32


def mix_bits(bits_in):
    bits_in = jnp.bitwise_xor(bits_in, lax.shift_right_logical(bits_in, jnp.int32(16)))
    bits_in = bits_in * jnp.int32(2146121005)
    bits_in = jnp.bitwise_xor(bits_in, lax.shift_right_logical(bits_in, jnp.int32(15)))
    bits_in = bits_in * jnp.int32(-2073254261)
    bits_in = jnp.bitwise_xor(bits_in, lax.shift_right_logical(bits_in, jnp.int32(16)))
    return bits_in


def unit_draw(seed_value, position):
    hashed = mix_bits(mix_bits(jnp.bitwise_xor(position, seed_value)) + seed_value)
    return (lax.shift_right_logical(hashed, jnp.int32(8)).astype(F32) + 0.5) * (1.0 / 16777216.0)


def gauss_noise(seed_value, position):
    draw_one = unit_draw(seed_value, 2 * position)
    draw_two = unit_draw(seed_value, 2 * position + 1)
    return jnp.sqrt(-2.0 * jnp.log(draw_one)) * jnp.cos(6.283185307179586 * draw_two)


def local_kernel(kernel, out_shape, flops, *operands):
    nbytes = sum(o.size * o.dtype.itemsize for o in operands[1:])
    nbytes += sum(o.size * o.dtype.itemsize for o in jax.tree.leaves(out_shape))
    vmem = pl.BlockSpec(memory_space=pltpu.VMEM)
    return pl.pallas_call(
        kernel,
        out_shape=out_shape,
        in_specs=[pl.BlockSpec(memory_space=pltpu.SMEM)] + [vmem] * (len(operands) - 1),
        out_specs=jax.tree.map(lambda _: vmem, out_shape),
        compiler_params=pltpu.CompilerParams(vmem_limit_bytes=40 << 20),
        cost_estimate=pl.CostEstimate(flops=flops, bytes_accessed=nbytes, transcendentals=0),
    )(*operands)


def as_row(block):
    return jnp.concatenate([block[i : i + 1, :] for i in range(block.shape[0])], axis=1)


def as_block(row, lanes):
    return jnp.concatenate(
        [row[:, i : i + lanes] for i in range(0, row.shape[1], lanes)], axis=0
    )


def as_column(row):
    return jnp.transpose(jnp.broadcast_to(row, (8, row.shape[1])))[:, :1]


def cot_columns(near_ref, far_ref, tokens):
    blocks = [ref[j, :tokens, :] for ref in (near_ref, far_ref) for j in range(ref.shape[0])]
    return jnp.concatenate(blocks, axis=1)


def sums_kernel(full_width, _, near_ref, far_ref, gram_ref, doc_col_ref, doc_row_ref, out_ref, inv_ref):
    tokens, lanes = gram_ref.shape[0], near_ref.shape[2]
    rows = tokens // lanes
    squares = jnp.zeros((rows, lanes), F32)
    for ref in (near_ref, far_ref):
        for j in range(ref.shape[0]):
            for term in range(3):
                start = tokens + term * rows
                squares = squares + ref[j, start : start + rows, :].astype(F32)
    inv = lax.rsqrt(squares / full_width + EPS_NORM)
    inv_ref[...] = inv
    inv_row = as_row(inv)
    inv_col = as_column(inv_row)
    cot = cot_columns(near_ref, far_ref, tokens)
    gram_values = lax.dot_general(cot, cot, (((1,), (1,)), ((), ())), preferred_element_type=F32)
    same_doc = doc_col_ref[...] == doc_row_ref[...]
    product = jnp.where(same_doc, gram_ref[...] * gram_values * inv_row, 0.0)
    row_sums = jnp.sum(product, axis=1, keepdims=True) * inv_col
    squared = jnp.sum(jnp.where(same_doc, row_sums, 0.0), axis=0, keepdims=True)
    packet = jnp.concatenate([as_block(squared, lanes), inv], axis=0)
    out_ref[...] = jnp.broadcast_to(packet[None], out_ref.shape)


def true_block(place_ref, j, n_blocks):
    mask, bit = 0, n_blocks // 2
    while bit:
        mask += bit * (j & 1)
        j //= 2
        bit //= 2
    return place_ref[0] ^ mask


def turn_kernel(group_rows, place_ref, near_ref, far_ref, near_other_ref, far_other_ref, out_ref):
    n_near, held, lanes = near_ref.shape
    width = out_ref.shape[0]
    tokens = out_ref.shape[1] // 2
    n_groups = width // group_rows
    places = []
    row = lax.broadcasted_iota(jnp.int32, (width, lanes), 0)
    lane = lax.broadcasted_iota(jnp.int32, (width, lanes), 1)
    for j in range(2 * n_near):
        kv = true_block(place_ref, j, 2 * n_near) * lanes + lane
        target = (kv % group_rows) * n_groups + kv // group_rows
        places.append(jnp.where(row == target, 1.0, 0.0).astype(BF16))
    places = jnp.concatenate(places, axis=1)
    for i, (near, far) in enumerate(((near_ref, far_ref), (near_other_ref, far_other_ref))):
        cot = cot_columns(near, far, tokens)
        out_ref[:, i * tokens : (i + 1) * tokens] = lax.dot_general(
            places, cot, (((1,), (1,)), ((), ())), preferred_element_type=F32
        ).astype(BF16)


def grad_kernel(place_ref, sums_ref, turned_ref, own_ref, other_ref, gain_ref, out_ref):
    n_all, rows_two, lanes = sums_ref.shape
    rows = rows_two // 2
    n_mp = n_all // 2
    tokens, half = own_ref.shape
    even = jnp.sum(sums_ref[:n_mp], axis=0)
    odd = jnp.sum(sums_ref[n_mp:], axis=0)
    even_inv, odd_inv = sums_ref[0], sums_ref[n_mp]
    first = place_ref[1] == 0
    normed, scales = [], []
    for near, far, near_inv, far_inv, ref in (
        (even, odd, even_inv, odd_inv, own_ref),
        (odd, even, odd_inv, even_inv, other_ref),
    ):
        squared = jnp.where(first, near, far)[:rows]
        inv_col = as_column(as_row(jnp.where(first, near_inv, far_inv)[rows:]))
        scales.append(CLIP_NORM / (jnp.sqrt(as_row(squared)) + 0.01))
        normed.append((ref[...].astype(F32) * inv_col * gain_ref[...]).astype(BF16))
    normed = jnp.concatenate(normed, axis=0)
    scales = jnp.concatenate(scales, axis=1)
    group_rows, n_groups = out_ref.shape[:2]
    step = max(1, group_rows // 4)
    for i in range(0, group_rows, step):
        rows_now = slice(i * n_groups, (i + step) * n_groups)
        clipped = (turned_ref[rows_now, :].astype(F32) * scales).astype(BF16)
        grad = jnp.dot(clipped, normed, preferred_element_type=F32).astype(BF16)
        out_ref[i : i + step] = grad.reshape(step, n_groups, half)


def back_kernel(
    n_yx, place_ref, near_ref, far_ref, weight_ref, weight_other_ref, input_ref, gain_ref, out_ref, inner_ref
):
    n_near, held, lanes = near_ref.shape
    tokens, width = input_ref.shape
    rows_half = weight_ref.shape[0]
    group_rows = rows_half // n_yx // 2
    col = lax.broadcasted_iota(jnp.int32, (lanes, 2 * rows_half), 1)
    lane = lax.broadcasted_iota(jnp.int32, (lanes, 2 * rows_half), 0)
    places = []
    for j in range(2 * n_near):
        kv = true_block(place_ref, j, 2 * n_near) * lanes + lane
        row, group = kv % group_rows, kv // group_rows
        core, plane, zh = group % 2, (group // 2) % n_yx, group // (2 * n_yx)
        core = jnp.where(core == place_ref[1], 0, 1)
        zh = jnp.where(zh == place_ref[2], 0, 1)
        target = core * rows_half + (plane * 2 + zh) * group_rows + row
        places.append(jnp.where(col == target, 1.0, 0.0).astype(BF16))
    places = jnp.concatenate(places, axis=0)
    cot = cot_columns(near_ref, far_ref, tokens)
    cot = jnp.dot(cot, places, preferred_element_type=F32).astype(BF16)
    inner = jnp.zeros((tokens, 1), F32)
    step = max(1, width // 4)
    for i in range(0, width, step):
        cols = slice(i, i + step)
        dnormed = jnp.dot(
            cot[:, :rows_half], weight_ref[:, cols], preferred_element_type=F32
        ) + jnp.dot(cot[:, rows_half:], weight_other_ref[:, cols], preferred_element_type=F32)
        weighted = gain_ref[:, cols] * dnormed
        out_ref[:, cols] = weighted
        inner = inner + jnp.sum(weighted * input_ref[:, cols].astype(F32), axis=1, keepdims=True)
    inner_row = jnp.transpose(jnp.broadcast_to(inner, (tokens, 8)))[:1, :]
    inner_ref[...] = jnp.broadcast_to(as_block(inner_row, lanes)[None], inner_ref.shape)


def body(
    layer_input,
    norm_gain,
    value_weight,
    value_cotangent,
    doc_ids,
    owners,
    noise_seeds,
    master,
    moment_one,
    moment_two,
):
    tokens, part_width = layer_input.shape
    cot_part = value_cotangent.shape[1]
    n_mp = lax.axis_size("mp")
    n_zh, n_core = lax.axis_size("zh"), lax.axis_size("core")
    n_yx = lax.axis_size("y") * lax.axis_size("x")
    full_width = part_width * n_mp
    group_rows = value_weight.shape[0]
    n_groups = owners.shape[0]
    value_width = n_groups * group_rows
    slots = master.shape[0] // group_rows
    half = part_width // n_core
    my_core = lax.axis_index("core")
    my_column = lax.axis_index("mp")
    my_zh = lax.axis_index("zh")
    my_yx = lax.axis_index(PLANE)
    my_group = lax.axis_index(DP_AXES)
    swap = [(0, 1), (1, 0)]

    inputs = layer_input.astype(F32)
    gain_row = norm_gain.astype(F32)[None, :]
    place = jnp.stack([my_column, my_core, my_zh]).astype(jnp.int32)

    squares_part = jnp.sum(inputs * inputs, axis=1)
    term_one = lax.reduce_precision(squares_part, 8, 7)
    rest = squares_part - term_one
    term_two = lax.reduce_precision(rest, 8, 7)
    terms = jnp.concatenate([term_one, term_two, rest - term_two]).astype(BF16)
    terms = terms.reshape(-1, cot_part)
    pad = jnp.zeros(((-terms.shape[0]) % 16, cot_part), BF16)
    near = jnp.concatenate([value_cotangent, terms, pad], axis=0)[None]
    weight_far = lax.ppermute(value_weight, "zh", swap)
    input_other = lax.ppermute(
        lax.dynamic_slice(layer_input, (0, (1 - my_core) * half), (tokens, half)), "core", swap
    )
    input_own = lax.dynamic_slice(layer_input, (0, my_core * half), (tokens, half))
    gained = (inputs * gain_row).astype(BF16)
    gram_features = jnp.dot(gained, gained.T, preferred_element_type=F32)
    doc_col, doc_row = doc_ids[:, None], doc_ids[None, :]
    bit = n_mp // 2
    while bit > 1:
        far = lax.ppermute(near, "mp", [(i, i ^ bit) for i in range(n_mp)])
        if bit == n_mp // 2:
            far, weight_far, input_own, input_other, doc_col, place = lax.optimization_barrier(
                (far, weight_far, input_own, input_other, doc_col, place)
            )
        else:
            far, gram_features = lax.optimization_barrier((far, gram_features))
        near = jnp.concatenate([near, far], axis=0)
        bit //= 2
    far = lax.ppermute(near, "mp", [(i, i ^ 1) for i in range(n_mp)])

    weight_pair = jnp.stack([value_weight, weight_far])
    weight_own = lax.all_to_all(
        jnp.broadcast_to(weight_pair[None], (n_yx,) + weight_pair.shape), PLANE, 0, 0
    ).reshape(value_width // n_core, part_width)
    far, weight_own = lax.optimization_barrier((far, weight_own))
    rows = tokens // cot_part
    sums_packet, inv_rms = local_kernel(
        functools.partial(sums_kernel, full_width),
        (
            jax.ShapeDtypeStruct((n_core * n_mp, 2 * rows, cot_part), F32),
            jax.ShapeDtypeStruct((rows, cot_part), F32),
        ),
        2 * tokens * tokens * value_width,
        place,
        near,
        far,
        gram_features,
        doc_col,
        doc_row,
    )
    sums_all = lax.all_to_all(sums_packet, ("core", "mp"), 0, 0)
    near_other = lax.ppermute(near, "core", swap)
    far, inv_rms = lax.optimization_barrier((far, inv_rms))
    far_other = lax.ppermute(far, "core", swap)
    turned = local_kernel(
        functools.partial(turn_kernel, group_rows),
        jax.ShapeDtypeStruct((value_width, n_core * tokens), BF16),
        4 * tokens * value_width * value_width,
        place,
        near,
        far,
        near_other,
        far_other,
    )
    sums_all, turned = lax.optimization_barrier((sums_all, turned))

    grad_rows = local_kernel(
        grad_kernel,
        jax.ShapeDtypeStruct((group_rows, n_groups, half), BF16),
        4 * tokens * value_width * half,
        place,
        sums_all,
        turned,
        input_own,
        input_other,
        lax.dynamic_slice(gain_row, (0, my_core * half), (1, half)),
    )
    grad_rows, weight_own = lax.optimization_barrier((grad_rows, weight_own))
    weight_other = lax.ppermute(weight_own, "core", swap)
    weighted, inner_packet = local_kernel(
        functools.partial(back_kernel, n_yx),
        (
            jax.ShapeDtypeStruct((tokens, part_width), F32),
            jax.ShapeDtypeStruct((n_mp, rows, cot_part), F32),
        ),
        4 * tokens * value_width * part_width,
        place,
        near,
        far,
        weight_own,
        weight_other,
        layer_input,
        gain_row,
    )

    grad_rows = lax.all_to_all(grad_rows, PLANE, 0, 0)
    grad_rows, inner_packet = lax.optimization_barrier((grad_rows, inner_packet))
    grad_plane = jnp.sum(grad_rows.astype(F32), axis=0)
    grad_far = lax.ppermute(grad_plane, "zh", swap)
    inner_sum = jnp.sum(lax.all_to_all(inner_packet, "mp", 0, 0), axis=0).reshape(tokens, 1)
    inv_col = inv_rms.reshape(tokens, 1)
    input_grad = (
        inv_col * weighted - inputs * inv_col * inv_col * inv_col * (inner_sum / full_width)
    ).astype(BF16)
    col_pos = my_column * part_width + my_core * half + jnp.arange(half, dtype=jnp.int32)[None, :]
    noise = gauss_noise(noise_seeds[:, None], my_yx * full_width + col_pos)
    noisy = grad_plane + grad_far + NOISE_MULT * CLIP_NORM * noise

    group_ids = jnp.arange(n_groups, dtype=jnp.int32)
    earlier = group_ids[:, None] > group_ids[None, :]
    same_owner = owners[:, None] == owners[None, :]
    slot_rank = jnp.sum((earlier & same_owner).astype(jnp.int32), axis=1)
    n_dest = n_groups // n_zh
    target = (owners - my_zh * n_dest) * slots + slot_rank
    places = jnp.arange(n_dest * slots, dtype=jnp.int32)
    sends = (places[:, None] == target[None, :]).astype(F32)
    outgoing = jnp.dot(sends, noisy, precision=lax.Precision.HIGHEST).reshape(n_dest, slots, half)
    arrived = lax.all_to_all(outgoing, PLANE + ("core",), 0, 0)
    gathered = (
        arrived.reshape(n_yx, n_core, slots, half)
        .transpose(2, 0, 1, 3)
        .reshape(slots * group_rows, part_width)
    )
    slot_ids = jnp.arange(slots, dtype=jnp.int32)
    filled = jnp.any(
        (owners[None, :] == my_group) & (slot_rank[None, :] == slot_ids[:, None]), axis=1
    )
    keep_mask = jnp.repeat(filled, group_rows)[:, None]
    first_new = BETA_ONE * moment_one + (1.0 - BETA_ONE) * gathered
    second_new = BETA_TWO * moment_two + (1.0 - BETA_TWO) * gathered * gathered
    update = (
        first_new
        / (1.0 - BETA_ONE**ADAM_STEP)
        / (jnp.sqrt(second_new / (1.0 - BETA_TWO**ADAM_STEP)) + ADAM_EPS)
    )
    new_master = jnp.where(keep_mask, master - LEARN_RATE * update, master)
    new_moment_one = jnp.where(keep_mask, first_new, moment_one)
    new_moment_two = jnp.where(keep_mask, second_new, moment_two)
    return (input_grad, new_master, new_moment_one, new_moment_two)


def solution(mesh, dp_split=DP_SPLIT):
    fine = Mesh(mesh.devices.reshape(dp_split + (mesh.shape["mp"],)), DP_AXES + ("mp",))
    rows, both = P(DP_AXES), P(DP_AXES, "mp")
    in_specs = (both, P("mp"), both, both, rows, P(), P(), both, both, both)
    out_specs = (both, both, both, both)
    return jax.shard_map(body, mesh=fine, in_specs=in_specs, out_specs=out_specs, check_vma=False)
```

```python
import functools

import jax
import jax.numpy as jnp
from jax import lax
from jax.experimental import pallas as pl
from jax.experimental.pallas import tpu as pltpu
from jax.sharding import Mesh
from jax.sharding import PartitionSpec as P

EPS_NORM = 1e-06
CLIP_NORM = 128.0
NOISE_MULT = 0.01
LEARN_RATE = 0.001
BETA_ONE = 0.9
BETA_TWO = 0.999
ADAM_STEP = 100
ADAM_EPS = 1e-08

DP_SPLIT = (2, 4, 4, 2)
DP_AXES = ("zh", "y", "x", "core")
PLANE = ("y", "x")
BF16 = jnp.bfloat16
F32 = jnp.float32


def mix_bits(bits_in):
    bits_in = jnp.bitwise_xor(bits_in, lax.shift_right_logical(bits_in, jnp.int32(16)))
    bits_in = bits_in * jnp.int32(2146121005)
    bits_in = jnp.bitwise_xor(bits_in, lax.shift_right_logical(bits_in, jnp.int32(15)))
    bits_in = bits_in * jnp.int32(-2073254261)
    bits_in = jnp.bitwise_xor(bits_in, lax.shift_right_logical(bits_in, jnp.int32(16)))
    return bits_in


def unit_draw(seed_value, position):
    hashed = mix_bits(mix_bits(jnp.bitwise_xor(position, seed_value)) + seed_value)
    return (lax.shift_right_logical(hashed, jnp.int32(8)).astype(F32) + 0.5) * (1.0 / 16777216.0)


def gauss_noise(seed_value, position):
    draw_one = unit_draw(seed_value, 2 * position)
    draw_two = unit_draw(seed_value, 2 * position + 1)
    return jnp.sqrt(-2.0 * jnp.log(draw_one)) * jnp.cos(6.283185307179586 * draw_two)


def local_kernel(kernel, out_shape, flops, *operands):
    nbytes = sum(o.size * o.dtype.itemsize for o in operands[1:])
    nbytes += sum(o.size * o.dtype.itemsize for o in jax.tree.leaves(out_shape))
    vmem = pl.BlockSpec(memory_space=pltpu.VMEM)
    return pl.pallas_call(
        kernel,
        out_shape=out_shape,
        in_specs=[pl.BlockSpec(memory_space=pltpu.SMEM)] + [vmem] * (len(operands) - 1),
        out_specs=jax.tree.map(lambda _: vmem, out_shape),
        compiler_params=pltpu.CompilerParams(vmem_limit_bytes=40 << 20),
        cost_estimate=pl.CostEstimate(flops=flops, bytes_accessed=nbytes, transcendentals=0),
    )(*operands)


def as_row(block):
    return jnp.concatenate([block[i : i + 1, :] for i in range(block.shape[0])], axis=1)


def as_block(row, lanes):
    return jnp.concatenate(
        [row[:, i : i + lanes] for i in range(0, row.shape[1], lanes)], axis=0
    )


def as_column(row):
    return jnp.transpose(jnp.broadcast_to(row, (8, row.shape[1])))[:, :1]


def cot_columns(refs, tokens):
    blocks = [ref[j, :tokens, :] for ref in refs for j in range(ref.shape[0])]
    return jnp.concatenate(blocks, axis=1)


def sums_kernel(
    full_width,
    _,
    near_ref,
    far_ref,
    gram_ref,
    values_ref,
    doc_col_ref,
    doc_row_ref,
    weight_ref,
    partial_ref,
    input_ref,
    gain_ref,
    out_ref,
    inv_ref,
    weighted_ref,
):
    tokens, lanes = gram_ref.shape[0], near_ref.shape[2]
    width = input_ref.shape[1]
    rows = tokens // lanes
    squares = jnp.zeros((rows, lanes), F32)
    for ref in (near_ref, far_ref):
        for j in range(ref.shape[0]):
            for term in range(3):
                start = tokens + term * rows
                squares = squares + ref[j, start : start + rows, :].astype(F32)
    inv = lax.rsqrt(squares / full_width + EPS_NORM)
    inv_ref[...] = inv
    inv_row = as_row(inv)
    inv_col = as_column(inv_row)
    cot = cot_columns((far_ref,), tokens)
    gram_values = values_ref[...] + lax.dot_general(
        cot, cot, (((1,), (1,)), ((), ())), preferred_element_type=F32
    )
    same_doc = doc_col_ref[...] == doc_row_ref[...]
    product = jnp.where(same_doc, gram_ref[...] * gram_values * inv_row, 0.0)
    row_sums = jnp.sum(product, axis=1, keepdims=True) * inv_col
    squared = jnp.sum(jnp.where(same_doc, row_sums, 0.0), axis=0, keepdims=True)
    inner = jnp.zeros((tokens, 1), F32)
    step = max(1, width // 4)
    for i in range(0, width, step):
        cols = slice(i, i + step)
        dnormed = partial_ref[:, cols] + jnp.dot(
            cot, weight_ref[:, cols], preferred_element_type=F32
        )
        weighted = gain_ref[:, cols] * dnormed
        weighted_ref[:, cols] = weighted
        inner = inner + jnp.sum(weighted * input_ref[:, cols].astype(F32), axis=1, keepdims=True)
    inner_row = jnp.transpose(jnp.broadcast_to(inner, (tokens, 8)))[:1, :]
    packet = jnp.concatenate(
        [as_block(squared, lanes), inv, as_block(inner_row, lanes), jnp.zeros((rows, lanes), F32)],
        axis=0,
    )
    out_ref[...] = jnp.broadcast_to(packet[None], out_ref.shape)


def true_block(place_ref, j, n_blocks):
    mask, bit = 0, n_blocks // 2
    while bit:
        mask += bit * (j & 1)
        j //= 2
        bit //= 2
    return place_ref[0] ^ mask


def turn_kernel(group_rows, place_ref, near_ref, far_ref, near_other_ref, far_other_ref, out_ref):
    n_near, held, lanes = near_ref.shape
    width = out_ref.shape[0]
    tokens = out_ref.shape[1] // 2
    n_groups = width // group_rows
    places = []
    row = lax.broadcasted_iota(jnp.int32, (width, lanes), 0)
    lane = lax.broadcasted_iota(jnp.int32, (width, lanes), 1)
    for j in range(2 * n_near):
        kv = true_block(place_ref, j, 2 * n_near) * lanes + lane
        target = (kv % group_rows) * n_groups + kv // group_rows
        places.append(jnp.where(row == target, 1.0, 0.0).astype(BF16))
    places = jnp.concatenate(places, axis=1)
    for i, (near, far) in enumerate(((near_ref, far_ref), (near_other_ref, far_other_ref))):
        cot = cot_columns((near, far), tokens)
        out_ref[:, i * tokens : (i + 1) * tokens] = lax.dot_general(
            places, cot, (((1,), (1,)), ((), ())), preferred_element_type=F32
        ).astype(BF16)


def grad_kernel(
    place_ref, sums_ref, turned_ref, own_ref, other_ref, gain_ref, out_ref, inner_ref
):
    n_all, rows_all, lanes = sums_ref.shape
    rows = rows_all // 4
    n_mp = n_all // 2
    tokens, half = own_ref.shape
    even = jnp.sum(sums_ref[:n_mp], axis=0)
    odd = jnp.sum(sums_ref[n_mp:], axis=0)
    even_inv, odd_inv = sums_ref[0], sums_ref[n_mp]
    first = place_ref[1] == 0
    normed, scales = [], []
    for near, far, near_inv, far_inv, ref in (
        (even, odd, even_inv, odd_inv, own_ref),
        (odd, even, odd_inv, even_inv, other_ref),
    ):
        squared = jnp.where(first, near, far)[:rows]
        inv_col = as_column(as_row(jnp.where(first, near_inv, far_inv)[rows : 2 * rows]))
        scales.append(CLIP_NORM / (jnp.sqrt(as_row(squared)) + 0.01))
        normed.append((ref[...].astype(F32) * inv_col * gain_ref[...]).astype(BF16))
    inner_ref[...] = jnp.where(first, even, odd)[2 * rows : 3 * rows]
    normed = jnp.concatenate(normed, axis=0)
    scales = jnp.concatenate(scales, axis=1)
    group_rows, n_groups = out_ref.shape[:2]
    step = max(1, group_rows // 4)
    for i in range(0, group_rows, step):
        rows_now = slice(i * n_groups, (i + step) * n_groups)
        clipped = (turned_ref[rows_now, :].astype(F32) * scales).astype(BF16)
        grad = jnp.dot(clipped, normed, preferred_element_type=F32).astype(BF16)
        out_ref[i : i + step] = grad.reshape(step, n_groups, half)


def near_kernel(
    n_yx, place_ref, near_ref, weight_ref, weight_other_ref, values_ref, partial_ref, far_weight_ref
):
    n_near, held, lanes = near_ref.shape
    tokens = values_ref.shape[0]
    rows_half, width = weight_ref.shape
    group_rows = rows_half // n_yx // 2
    cot = cot_columns((near_ref,), tokens)
    values_ref[...] = lax.dot_general(
        cot, cot, (((1,), (1,)), ((), ())), preferred_element_type=F32
    )
    target = lax.broadcasted_iota(jnp.int32, (lanes, 2 * rows_half), 1)
    lane = lax.broadcasted_iota(jnp.int32, (lanes, 2 * rows_half), 0)
    ordered = []
    for j in range(2 * n_near):
        kv = true_block(place_ref, j, 2 * n_near) * lanes + lane
        row, group = kv % group_rows, kv // group_rows
        core, plane, zh = group % 2, (group // 2) % n_yx, group // (2 * n_yx)
        core = jnp.where(core == place_ref[1], 0, 1)
        zh = jnp.where(zh == place_ref[2], 0, 1)
        source = core * rows_half + (plane * 2 + zh) * group_rows + row
        ordered.append(jnp.where(target == source, 1.0, 0.0).astype(BF16))
    for first in (True, False):
        places = jnp.concatenate(ordered[:n_near] if first else ordered[n_near:], axis=0)
        rows_now = (
            jnp.dot(places[:, :rows_half], weight_ref[...], preferred_element_type=F32)
            + jnp.dot(places[:, rows_half:], weight_other_ref[...], preferred_element_type=F32)
        ).astype(BF16)
        if first:
            partial_ref[...] = jnp.dot(cot, rows_now, preferred_element_type=F32)
        else:
            far_weight_ref[...] = rows_now


def body(
    layer_input,
    norm_gain,
    value_weight,
    value_cotangent,
    doc_ids,
    owners,
    noise_seeds,
    master,
    moment_one,
    moment_two,
):
    tokens, part_width = layer_input.shape
    cot_part = value_cotangent.shape[1]
    n_mp = lax.axis_size("mp")
    n_zh, n_core = lax.axis_size("zh"), lax.axis_size("core")
    n_yx = lax.axis_size("y") * lax.axis_size("x")
    full_width = part_width * n_mp
    group_rows = value_weight.shape[0]
    n_groups = owners.shape[0]
    value_width = n_groups * group_rows
    slots = master.shape[0] // group_rows
    half = part_width // n_core
    my_core = lax.axis_index("core")
    my_column = lax.axis_index("mp")
    my_zh = lax.axis_index("zh")
    my_yx = lax.axis_index(PLANE)
    my_group = lax.axis_index(DP_AXES)
    swap = [(0, 1), (1, 0)]

    inputs = layer_input.astype(F32)
    gain_row = norm_gain.astype(F32)[None, :]
    place = jnp.stack([my_column, my_core, my_zh]).astype(jnp.int32)

    squares_part = jnp.sum(inputs * inputs, axis=1)
    term_one = lax.reduce_precision(squares_part, 8, 7)
    rest = squares_part - term_one
    term_two = lax.reduce_precision(rest, 8, 7)
    terms = jnp.concatenate([term_one, term_two, rest - term_two]).astype(BF16)
    terms = terms.reshape(-1, cot_part)
    pad = jnp.zeros(((-terms.shape[0]) % 16, cot_part), BF16)
    near = jnp.concatenate([value_cotangent, terms, pad], axis=0)[None]
    weight_far = lax.ppermute(value_weight, "zh", swap)
    input_own = lax.dynamic_slice(layer_input, (0, my_core * half), (tokens, half))
    input_other = lax.dynamic_slice(layer_input, (0, (1 - my_core) * half), (tokens, half))
    near, weight_far, input_own, input_other = lax.optimization_barrier(
        (near, weight_far, input_own, input_other)
    )
    input_other = lax.ppermute(input_other, "core", swap)
    gained = (inputs * gain_row).astype(BF16)
    gram_features = jnp.dot(gained, gained.T, preferred_element_type=F32)
    doc_col, doc_row = doc_ids[:, None], doc_ids[None, :]
    bit = n_mp // 2
    while bit > 1:
        far = lax.ppermute(near, "mp", [(i, i ^ bit) for i in range(n_mp)])
        if bit == n_mp // 2:
            far, doc_col, place = lax.optimization_barrier((far, doc_col, place))
        else:
            far, gram_features = lax.optimization_barrier((far, gram_features))
        near = jnp.concatenate([near, far], axis=0)
        bit //= 2
    weight_pair = jnp.stack([value_weight, weight_far])
    weight_own = lax.all_to_all(
        jnp.broadcast_to(weight_pair[None], (n_yx,) + weight_pair.shape), PLANE, 0, 0
    ).reshape(value_width // n_core, part_width)
    weight_other = lax.ppermute(weight_own, "core", swap)

    far = lax.ppermute(near, "mp", [(i, i ^ 1) for i in range(n_mp)])
    near_other = lax.ppermute(near, "core", swap)
    near_values, near_partial, far_weight = local_kernel(
        functools.partial(near_kernel, n_yx),
        (
            jax.ShapeDtypeStruct((tokens, tokens), F32),
            jax.ShapeDtypeStruct((tokens, part_width), F32),
            jax.ShapeDtypeStruct((value_width // 2, part_width), BF16),
        ),
        6 * tokens * value_width * part_width,
        place,
        near,
        weight_own,
        weight_other,
    )
    far, near_values, near_other = lax.optimization_barrier((far, near_values, near_other))

    rows = tokens // cot_part
    sums_packet, inv_rms, weighted = local_kernel(
        functools.partial(sums_kernel, full_width),
        (
            jax.ShapeDtypeStruct((n_core * n_mp, 4 * rows, cot_part), F32),
            jax.ShapeDtypeStruct((rows, cot_part), F32),
            jax.ShapeDtypeStruct((tokens, part_width), F32),
        ),
        2 * tokens * tokens * value_width,
        place,
        near,
        far,
        gram_features,
        near_values,
        doc_col,
        doc_row,
        far_weight,
        near_partial,
        layer_input,
        gain_row,
    )
    sums_all = lax.all_to_all(sums_packet, ("core", "mp"), 0, 0)
    far, inv_rms = lax.optimization_barrier((far, inv_rms))
    far_other = lax.ppermute(far, "core", swap)
    turned = local_kernel(
        functools.partial(turn_kernel, group_rows),
        jax.ShapeDtypeStruct((value_width, n_core * tokens), BF16),
        4 * tokens * value_width * value_width,
        place,
        near,
        far,
        near_other,
        far_other,
    )
    sums_all, turned = lax.optimization_barrier((sums_all, turned))

    grad_rows, inner_sum = local_kernel(
        grad_kernel,
        (
            jax.ShapeDtypeStruct((group_rows, n_groups, half), BF16),
            jax.ShapeDtypeStruct((rows, cot_part), F32),
        ),
        4 * tokens * value_width * half,
        place,
        sums_all,
        turned,
        input_own,
        input_other,
        lax.dynamic_slice(gain_row, (0, my_core * half), (1, half)),
    )
    inv_col = inv_rms.reshape(tokens, 1)
    input_grad = (
        inv_col * weighted
        - inputs * inv_col * inv_col * inv_col * (inner_sum.reshape(tokens, 1) / full_width)
    ).astype(BF16)
    grad_rows = lax.all_to_all(grad_rows, PLANE, 0, 0)
    grad_plane = jnp.sum(grad_rows.astype(F32), axis=0)
    grad_far = lax.ppermute(grad_plane, "zh", swap)
    col_pos = my_column * part_width + my_core * half + jnp.arange(half, dtype=jnp.int32)[None, :]
    noise = gauss_noise(noise_seeds[:, None], my_yx * full_width + col_pos)
    noisy = grad_plane + grad_far + NOISE_MULT * CLIP_NORM * noise

    group_ids = jnp.arange(n_groups, dtype=jnp.int32)
    earlier = group_ids[:, None] > group_ids[None, :]
    same_owner = owners[:, None] == owners[None, :]
    slot_rank = jnp.sum((earlier & same_owner).astype(jnp.int32), axis=1)
    n_dest = n_groups // n_zh
    target = (owners - my_zh * n_dest) * slots + slot_rank
    places = jnp.arange(n_dest * slots, dtype=jnp.int32)
    sends = (places[:, None] == target[None, :]).astype(F32)
    outgoing = jnp.dot(sends, noisy, precision=lax.Precision.HIGHEST).reshape(n_dest, slots, half)
    arrived = lax.all_to_all(outgoing, PLANE + ("core",), 0, 0)
    gathered = (
        arrived.reshape(n_yx, n_core, slots, half)
        .transpose(2, 0, 1, 3)
        .reshape(slots * group_rows, part_width)
    )
    slot_ids = jnp.arange(slots, dtype=jnp.int32)
    filled = jnp.any(
        (owners[None, :] == my_group) & (slot_rank[None, :] == slot_ids[:, None]), axis=1
    )
    keep_mask = jnp.repeat(filled, group_rows)[:, None]
    first_new = BETA_ONE * moment_one + (1.0 - BETA_ONE) * gathered
    second_new = BETA_TWO * moment_two + (1.0 - BETA_TWO) * gathered * gathered
    update = (
        first_new
        / (1.0 - BETA_ONE**ADAM_STEP)
        / (jnp.sqrt(second_new / (1.0 - BETA_TWO**ADAM_STEP)) + ADAM_EPS)
    )
    new_master = jnp.where(keep_mask, master - LEARN_RATE * update, master)
    new_moment_one = jnp.where(keep_mask, first_new, moment_one)
    new_moment_two = jnp.where(keep_mask, second_new, moment_two)
    return (input_grad, new_master, new_moment_one, new_moment_two)


def solution(mesh, dp_split=DP_SPLIT):
    fine = Mesh(mesh.devices.reshape(dp_split + (mesh.shape["mp"],)), DP_AXES + ("mp",))
    rows, both = P(DP_AXES), P(DP_AXES, "mp")
    in_specs = (both, P("mp"), both, both, rows, P(), P(), both, both, both)
    out_specs = (both, both, both, both)
    return jax.shard_map(body, mesh=fine, in_specs=in_specs, out_specs=out_specs, check_vma=False)
```

```python
import functools

import jax
import jax.numpy as jnp
from jax import lax
from jax.experimental import pallas as pl
from jax.experimental.pallas import tpu as pltpu
from jax.sharding import Mesh
from jax.sharding import PartitionSpec as P

EPS_NORM = 1e-06
CLIP_NORM = 128.0
NOISE_MULT = 0.01
LEARN_RATE = 0.001
BETA_ONE = 0.9
BETA_TWO = 0.999
ADAM_STEP = 100
ADAM_EPS = 1e-08

DP_SPLIT = (2, 4, 4, 2)
DP_AXES = ("zh", "y", "x", "core")
PLANE = ("y", "x")
BF16 = jnp.bfloat16
F32 = jnp.float32


def mix_bits(bits_in):
    bits_in = jnp.bitwise_xor(bits_in, lax.shift_right_logical(bits_in, jnp.int32(16)))
    bits_in = bits_in * jnp.int32(2146121005)
    bits_in = jnp.bitwise_xor(bits_in, lax.shift_right_logical(bits_in, jnp.int32(15)))
    bits_in = bits_in * jnp.int32(-2073254261)
    bits_in = jnp.bitwise_xor(bits_in, lax.shift_right_logical(bits_in, jnp.int32(16)))
    return bits_in


def unit_draw(seed_value, position):
    hashed = mix_bits(mix_bits(jnp.bitwise_xor(position, seed_value)) + seed_value)
    return (lax.shift_right_logical(hashed, jnp.int32(8)).astype(F32) + 0.5) * (1.0 / 16777216.0)


def gauss_noise(seed_value, position):
    draw_one = unit_draw(seed_value, 2 * position)
    draw_two = unit_draw(seed_value, 2 * position + 1)
    return jnp.sqrt(-2.0 * jnp.log(draw_one)) * jnp.cos(6.283185307179586 * draw_two)


def local_kernel(kernel, out_shape, flops, *operands):
    nbytes = sum(o.size * o.dtype.itemsize for o in operands[1:])
    nbytes += sum(o.size * o.dtype.itemsize for o in jax.tree.leaves(out_shape))
    vmem = pl.BlockSpec(memory_space=pltpu.VMEM)
    return pl.pallas_call(
        kernel,
        out_shape=out_shape,
        in_specs=[pl.BlockSpec(memory_space=pltpu.SMEM)] + [vmem] * (len(operands) - 1),
        out_specs=jax.tree.map(lambda _: vmem, out_shape),
        compiler_params=pltpu.CompilerParams(vmem_limit_bytes=40 << 20),
        cost_estimate=pl.CostEstimate(flops=flops, bytes_accessed=nbytes, transcendentals=0),
    )(*operands)


def as_row(block):
    return jnp.concatenate([block[i : i + 1, :] for i in range(block.shape[0])], axis=1)


def as_block(row, lanes):
    return jnp.concatenate(
        [row[:, i : i + lanes] for i in range(0, row.shape[1], lanes)], axis=0
    )


def as_column(row):
    return jnp.transpose(jnp.broadcast_to(row, (8, row.shape[1])))[:, :1]


def cot_columns(refs, tokens):
    blocks = [ref[j, :tokens, :] for ref in refs for j in range(ref.shape[0])]
    return jnp.concatenate(blocks, axis=1)


def true_blocks(place_ref, masks):
    return [place_ref[0] ^ mask for mask in masks]


def sums_kernel(full_width, _, first, second, third, last, gram_ref, doc_col_ref, doc_row_ref, out_ref, inv_ref):
    tokens, lanes = gram_ref.shape[0], first.shape[2]
    rows = tokens // lanes
    squares = jnp.zeros((rows, lanes), F32)
    for ref in (first, second, third, last):
        for j in range(ref.shape[0]):
            for term in range(3):
                start = tokens + term * rows
                squares = squares + ref[j, start : start + rows, :].astype(F32)
    inv = lax.rsqrt(squares / full_width + EPS_NORM)
    inv_ref[...] = inv
    inv_row = as_row(inv)
    inv_col = as_column(inv_row)
    cot = cot_columns((first, second, third, last), tokens)
    gram_values = lax.dot_general(cot, cot, (((1,), (1,)), ((), ())), preferred_element_type=F32)
    same_doc = doc_col_ref[...] == doc_row_ref[...]
    product = jnp.where(same_doc, gram_ref[...] * gram_values * inv_row, 0.0)
    row_sums = jnp.sum(product, axis=1, keepdims=True) * inv_col
    squared = jnp.sum(jnp.where(same_doc, row_sums, 0.0), axis=0, keepdims=True)
    packet = jnp.concatenate([as_block(squared, lanes), inv], axis=0)
    out_ref[...] = jnp.broadcast_to(packet[None], out_ref.shape)


def turn_kernel(group_rows, masks, place_ref, first, second, third, last, out_ref):
    lanes = first.shape[2]
    width, tokens = out_ref.shape
    n_groups = width // group_rows
    places = []
    row = lax.broadcasted_iota(jnp.int32, (width, lanes), 0)
    lane = lax.broadcasted_iota(jnp.int32, (width, lanes), 1)
    for block in true_blocks(place_ref, masks):
        kv = block * lanes + lane
        target = (kv % group_rows) * n_groups + kv // group_rows
        places.append(jnp.where(row == target, 1.0, 0.0).astype(BF16))
    places = jnp.concatenate(places, axis=1)
    cot = cot_columns((first, second, third, last), tokens)
    out_ref[...] = lax.dot_general(
        places, cot, (((1,), (1,)), ((), ())), preferred_element_type=F32
    ).astype(BF16)


def grad_kernel(place_ref, sums_ref, turned_ref, turned_other_ref, own_ref, other_ref, gain_ref, out_ref):
    n_all, rows_two, lanes = sums_ref.shape
    rows = rows_two // 2
    n_mp = n_all // 2
    tokens, half = own_ref.shape
    even = jnp.sum(sums_ref[:n_mp], axis=0)
    odd = jnp.sum(sums_ref[n_mp:], axis=0)
    even_inv, odd_inv = sums_ref[0], sums_ref[n_mp]
    first = place_ref[1] == 0
    normed, scales = [], []
    for near, far, near_inv, far_inv, ref in (
        (even, odd, even_inv, odd_inv, own_ref),
        (odd, even, odd_inv, even_inv, other_ref),
    ):
        squared = jnp.where(first, near, far)[:rows]
        inv_col = as_column(as_row(jnp.where(first, near_inv, far_inv)[rows:]))
        scales.append(CLIP_NORM / (jnp.sqrt(as_row(squared)) + 0.01))
        normed.append((ref[...].astype(F32) * inv_col * gain_ref[...]).astype(BF16))
    normed = jnp.concatenate(normed, axis=0)
    group_rows, n_groups = out_ref.shape[:2]
    step = max(1, group_rows // 4)
    for i in range(0, group_rows, step):
        rows_now = slice(i * n_groups, (i + step) * n_groups)
        clipped = jnp.concatenate(
            [
                (ref[rows_now, :].astype(F32) * scale).astype(BF16)
                for ref, scale in zip((turned_ref, turned_other_ref), scales)
            ],
            axis=1,
        )
        grad = jnp.dot(clipped, normed, preferred_element_type=F32).astype(BF16)
        out_ref[i : i + step] = grad.reshape(step, n_groups, half)


def back_kernel(
    n_yx, masks, place_ref, first, second, third, last, weight_ref, input_ref, gain_ref, out_ref, inner_ref
):
    lanes = first.shape[2]
    tokens, width = input_ref.shape
    n_rows = weight_ref.shape[0]
    group_rows = n_rows // n_yx // 4
    col = lax.broadcasted_iota(jnp.int32, (lanes, n_rows), 1)
    lane = lax.broadcasted_iota(jnp.int32, (lanes, n_rows), 0)
    places = []
    for block in true_blocks(place_ref, masks):
        kv = block * lanes + lane
        row, group = kv % group_rows, kv // group_rows
        core, plane, zh = group % 2, (group // 2) % n_yx, group // (2 * n_yx)
        zh = jnp.where(zh == place_ref[2], 0, 1)
        target = ((plane * 2 + core) * 2 + zh) * group_rows + row
        places.append(jnp.where(col == target, 1.0, 0.0).astype(BF16))
    places = jnp.concatenate(places, axis=0)
    cot = cot_columns((first, second, third, last), tokens)
    cot = jnp.dot(cot, places, preferred_element_type=F32).astype(BF16)
    inner = jnp.zeros((tokens, 1), F32)
    step = max(1, width // 4)
    for i in range(0, width, step):
        cols = slice(i, i + step)
        weighted = gain_ref[:, cols] * jnp.dot(cot, weight_ref[:, cols], preferred_element_type=F32)
        out_ref[:, cols] = weighted
        inner = inner + jnp.sum(weighted * input_ref[:, cols].astype(F32), axis=1, keepdims=True)
    inner_row = jnp.transpose(jnp.broadcast_to(inner, (tokens, 8)))[:1, :]
    inner_ref[...] = as_block(inner_row, lanes)


def body(
    layer_input,
    norm_gain,
    value_weight,
    value_cotangent,
    doc_ids,
    owners,
    noise_seeds,
    master,
    moment_one,
    moment_two,
):
    tokens, part_width = layer_input.shape
    cot_part = value_cotangent.shape[1]
    n_mp = lax.axis_size("mp")
    n_zh, n_core = lax.axis_size("zh"), lax.axis_size("core")
    n_yx = lax.axis_size("y") * lax.axis_size("x")
    full_width = part_width * n_mp
    group_rows = value_weight.shape[0]
    n_groups = owners.shape[0]
    value_width = n_groups * group_rows
    slots = master.shape[0] // group_rows
    half = part_width // n_core
    my_core = lax.axis_index("core")
    my_column = lax.axis_index("mp")
    my_zh = lax.axis_index("zh")
    my_yx = lax.axis_index(PLANE)
    my_group = lax.axis_index(DP_AXES)
    swap = [(0, 1), (1, 0)]

    inputs = layer_input.astype(F32)
    gain_row = norm_gain.astype(F32)[None, :]
    place = jnp.stack([my_column, my_core, my_zh]).astype(jnp.int32)

    squares_part = jnp.sum(inputs * inputs, axis=1)
    term_one = lax.reduce_precision(squares_part, 8, 7)
    rest = squares_part - term_one
    term_two = lax.reduce_precision(rest, 8, 7)
    terms = jnp.concatenate([term_one, term_two, rest - term_two]).astype(BF16)
    terms = terms.reshape(-1, cot_part)
    pad = jnp.zeros(((-terms.shape[0]) % 16, cot_part), BF16)
    packet = jnp.concatenate([value_cotangent, terms, pad], axis=0)[None]

    def across(array, bit):
        return lax.ppermute(array, "mp", [(i, i ^ bit) for i in range(n_mp)])

    top, middle = n_mp // 2, n_mp // 4
    masks = [0, top, middle, middle + top, 1, 1 + top, 1 + middle, 1 + middle + top]
    weight_far = lax.ppermute(value_weight, "zh", swap)
    input_other = lax.ppermute(
        lax.dynamic_slice(layer_input, (0, (1 - my_core) * half), (tokens, half)), "core", swap
    )
    input_own = lax.dynamic_slice(layer_input, (0, my_core * half), (tokens, half))
    doc_col, doc_row = doc_ids[:, None], doc_ids[None, :]
    packet_far = across(packet, top)
    packet_far, weight_far, input_own, input_other, doc_col, place = lax.optimization_barrier(
        (packet_far, weight_far, input_own, input_other, doc_col, place)
    )
    first = jnp.concatenate([packet, packet_far], axis=0)
    second, third = across(first, middle), across(first, 1)
    gained = (inputs * gain_row).astype(BF16)
    gram_features = jnp.dot(gained, gained.T, preferred_element_type=F32)
    second, third, gram_features = lax.optimization_barrier((second, third, gram_features))
    last = across(second, 1)

    weight_pair = jnp.concatenate([value_weight, weight_far], axis=0)
    full_weight = lax.all_gather(weight_pair, PLANE + ("core",), axis=0, tiled=True)

    rows = tokens // cot_part
    sums_packet, inv_rms = local_kernel(
        functools.partial(sums_kernel, full_width),
        (
            jax.ShapeDtypeStruct((n_core * n_mp, 2 * rows, cot_part), F32),
            jax.ShapeDtypeStruct((rows, cot_part), F32),
        ),
        2 * tokens * tokens * value_width,
        place,
        first,
        second,
        third,
        last,
        gram_features,
        doc_col,
        doc_row,
    )
    sums_all = lax.all_to_all(sums_packet, ("core", "mp"), 0, 0)
    last, inv_rms = lax.optimization_barrier((last, inv_rms))
    turned = local_kernel(
        functools.partial(turn_kernel, group_rows, masks),
        jax.ShapeDtypeStruct((value_width, tokens), BF16),
        2 * tokens * value_width * value_width,
        place,
        first,
        second,
        third,
        last,
    )
    turned_other = lax.ppermute(turned, "core", swap)
    sums_all, turned, turned_other = lax.optimization_barrier((sums_all, turned, turned_other))

    grad_rows = local_kernel(
        grad_kernel,
        jax.ShapeDtypeStruct((group_rows, n_groups, half), BF16),
        4 * tokens * value_width * half,
        place,
        sums_all,
        turned,
        turned_other,
        input_own,
        input_other,
        lax.dynamic_slice(gain_row, (0, my_core * half), (1, half)),
    )
    grad_rows, last = lax.optimization_barrier((grad_rows, last))
    weighted, inner_sum = local_kernel(
        functools.partial(back_kernel, n_yx, masks),
        (
            jax.ShapeDtypeStruct((tokens, part_width), F32),
            jax.ShapeDtypeStruct((rows, cot_part), F32),
        ),
        4 * tokens * value_width * part_width,
        place,
        first,
        second,
        third,
        last,
        full_weight,
        layer_input,
        gain_row,
    )
    grad_rows = lax.all_to_all(grad_rows, PLANE, 0, 0)
    grad_rows, inner_sum = lax.optimization_barrier((grad_rows, inner_sum))
    for bit in (1, middle, top):
        inner_sum = inner_sum + across(inner_sum, bit)
    inv_col = inv_rms.reshape(tokens, 1)
    input_grad = (
        inv_col * weighted
        - inputs * inv_col * inv_col * inv_col * (inner_sum.reshape(tokens, 1) / full_width)
    ).astype(BF16)

    grad_plane = jnp.sum(grad_rows.astype(F32), axis=0)
    col_pos = my_column * part_width + my_core * half + jnp.arange(half, dtype=jnp.int32)[None, :]
    noise = gauss_noise(noise_seeds[:, None], my_yx * full_width + col_pos)
    noisy = grad_plane + jnp.where(my_zh == 0, NOISE_MULT * CLIP_NORM, 0.0) * noise

    group_ids = jnp.arange(n_groups, dtype=jnp.int32)
    earlier = group_ids[:, None] > group_ids[None, :]
    same_owner = owners[:, None] == owners[None, :]
    slot_rank = jnp.sum((earlier & same_owner).astype(jnp.int32), axis=1)
    target = owners * slots + slot_rank
    places = jnp.arange(n_groups * slots, dtype=jnp.int32)
    sends = (places[:, None] == target[None, :]).astype(F32)
    outgoing = jnp.dot(sends, noisy, precision=lax.Precision.HIGHEST).astype(BF16)
    arrived = lax.all_to_all(outgoing.reshape(n_groups, slots, half), DP_AXES, 0, 0)
    gathered = (
        jnp.sum(arrived.reshape(n_zh, n_yx, n_core, slots, half).astype(F32), axis=0)
        .transpose(2, 0, 1, 3)
        .reshape(slots * group_rows, part_width)
    )
    slot_ids = jnp.arange(slots, dtype=jnp.int32)
    filled = jnp.any(
        (owners[None, :] == my_group) & (slot_rank[None, :] == slot_ids[:, None]), axis=1
    )
    keep_mask = jnp.repeat(filled, group_rows)[:, None]
    first_new = BETA_ONE * moment_one + (1.0 - BETA_ONE) * gathered
    second_new = BETA_TWO * moment_two + (1.0 - BETA_TWO) * gathered * gathered
    update = (
        first_new
        / (1.0 - BETA_ONE**ADAM_STEP)
        / (jnp.sqrt(second_new / (1.0 - BETA_TWO**ADAM_STEP)) + ADAM_EPS)
    )
    new_master = jnp.where(keep_mask, master - LEARN_RATE * update, master)
    new_moment_one = jnp.where(keep_mask, first_new, moment_one)
    new_moment_two = jnp.where(keep_mask, second_new, moment_two)
    return (input_grad, new_master, new_moment_one, new_moment_two)


def solution(mesh, dp_split=DP_SPLIT):
    fine = Mesh(mesh.devices.reshape(dp_split + (mesh.shape["mp"],)), DP_AXES + ("mp",))
    rows, both = P(DP_AXES), P(DP_AXES, "mp")
    in_specs = (both, P("mp"), both, both, rows, P(), P(), both, both, both)
    out_specs = (both, both, both, both)
    return jax.shard_map(body, mesh=fine, in_specs=in_specs, out_specs=out_specs, check_vma=False)
```

```python
import functools

import jax
import jax.numpy as jnp
from jax import lax
from jax.experimental import pallas as pl
from jax.experimental.pallas import tpu as pltpu
from jax.sharding import Mesh
from jax.sharding import PartitionSpec as P

EPS_NORM = 1e-06
CLIP_NORM = 128.0
NOISE_MULT = 0.01
LEARN_RATE = 0.001
BETA_ONE = 0.9
BETA_TWO = 0.999
ADAM_STEP = 100
ADAM_EPS = 1e-08

DP_SPLIT = (2, 4, 4, 2)
DP_AXES = ("zh", "y", "x", "core")
PLANE = ("y", "x")
BF16 = jnp.bfloat16
F32 = jnp.float32


def mix_bits(bits_in):
    bits_in = jnp.bitwise_xor(bits_in, lax.shift_right_logical(bits_in, jnp.int32(16)))
    bits_in = bits_in * jnp.int32(2146121005)
    bits_in = jnp.bitwise_xor(bits_in, lax.shift_right_logical(bits_in, jnp.int32(15)))
    bits_in = bits_in * jnp.int32(-2073254261)
    bits_in = jnp.bitwise_xor(bits_in, lax.shift_right_logical(bits_in, jnp.int32(16)))
    return bits_in


def unit_draw(seed_value, position):
    hashed = mix_bits(mix_bits(jnp.bitwise_xor(position, seed_value)) + seed_value)
    return (lax.shift_right_logical(hashed, jnp.int32(8)).astype(F32) + 0.5) * (1.0 / 16777216.0)


def gauss_noise(seed_value, position):
    draw_one = unit_draw(seed_value, 2 * position)
    draw_two = unit_draw(seed_value, 2 * position + 1)
    return jnp.sqrt(-2.0 * jnp.log(draw_one)) * jnp.cos(6.283185307179586 * draw_two)


def local_kernel(kernel, out_shape, flops, *operands):
    nbytes = sum(o.size * o.dtype.itemsize for o in operands[1:])
    nbytes += sum(o.size * o.dtype.itemsize for o in jax.tree.leaves(out_shape))
    vmem = pl.BlockSpec(memory_space=pltpu.VMEM)
    return pl.pallas_call(
        kernel,
        out_shape=out_shape,
        in_specs=[pl.BlockSpec(memory_space=pltpu.SMEM)] + [vmem] * (len(operands) - 1),
        out_specs=jax.tree.map(lambda _: vmem, out_shape),
        compiler_params=pltpu.CompilerParams(vmem_limit_bytes=40 << 20),
        cost_estimate=pl.CostEstimate(flops=flops, bytes_accessed=nbytes, transcendentals=0),
    )(*operands)


def as_row(block):
    return jnp.concatenate([block[i : i + 1, :] for i in range(block.shape[0])], axis=1)


def as_block(row, lanes):
    return jnp.concatenate(
        [row[:, i : i + lanes] for i in range(0, row.shape[1], lanes)], axis=0
    )


def as_column(row):
    return jnp.transpose(jnp.broadcast_to(row, (8, row.shape[1])))[:, :1]


def cot_columns(refs, tokens):
    blocks = [ref[j, :tokens, :] for ref in refs for j in range(ref.shape[0])]
    return jnp.concatenate(blocks, axis=1)


def true_blocks(place_ref, masks):
    return [place_ref[0] ^ mask for mask in masks]


def sums_kernel(full_width, _, first, second, third, last, gram_ref, doc_col_ref, doc_row_ref, out_ref, inv_ref):
    tokens, lanes = gram_ref.shape[0], first.shape[2]
    rows = tokens // lanes
    squares = jnp.zeros((rows, lanes), F32)
    for ref in (first, second, third, last):
        for j in range(ref.shape[0]):
            for term in range(3):
                start = tokens + term * rows
                squares = squares + ref[j, start : start + rows, :].astype(F32)
    inv = lax.rsqrt(squares / full_width + EPS_NORM)
    inv_ref[...] = inv
    inv_row = as_row(inv)
    inv_col = as_column(inv_row)
    cot = cot_columns((first, second, third, last), tokens)
    gram_values = lax.dot_general(cot, cot, (((1,), (1,)), ((), ())), preferred_element_type=F32)
    same_doc = doc_col_ref[...] == doc_row_ref[...]
    product = jnp.where(same_doc, gram_ref[...] * gram_values * inv_row, 0.0)
    row_sums = jnp.sum(product, axis=1, keepdims=True) * inv_col
    squared = jnp.sum(jnp.where(same_doc, row_sums, 0.0), axis=0, keepdims=True)
    packet = jnp.concatenate([as_block(squared, lanes), inv], axis=0)
    out_ref[...] = jnp.broadcast_to(packet[None], out_ref.shape)


def turn_kernel(group_rows, masks, place_ref, first, second, third, last, out_ref):
    lanes = first.shape[2]
    width, tokens = out_ref.shape
    n_groups = width // group_rows
    places = []
    row = lax.broadcasted_iota(jnp.int32, (width, lanes), 0)
    lane = lax.broadcasted_iota(jnp.int32, (width, lanes), 1)
    for block in true_blocks(place_ref, masks):
        kv = block * lanes + lane
        target = (kv % group_rows) * n_groups + kv // group_rows
        places.append(jnp.where(row == target, 1.0, 0.0).astype(BF16))
    places = jnp.concatenate(places, axis=1)
    cot = cot_columns((first, second, third, last), tokens)
    out_ref[...] = lax.dot_general(
        places, cot, (((1,), (1,)), ((), ())), preferred_element_type=F32
    ).astype(BF16)


def grad_kernel(place_ref, sums_ref, turned_ref, turned_other_ref, own_ref, other_ref, gain_ref, out_ref):
    n_all, rows_two, lanes = sums_ref.shape
    rows = rows_two // 2
    n_mp = n_all // 2
    tokens, half = own_ref.shape
    even = jnp.sum(sums_ref[:n_mp], axis=0)
    odd = jnp.sum(sums_ref[n_mp:], axis=0)
    even_inv, odd_inv = sums_ref[0], sums_ref[n_mp]
    first = place_ref[1] == 0
    normed, scales = [], []
    for near, far, near_inv, far_inv, ref in (
        (even, odd, even_inv, odd_inv, own_ref),
        (odd, even, odd_inv, even_inv, other_ref),
    ):
        squared = jnp.where(first, near, far)[:rows]
        inv_col = as_column(as_row(jnp.where(first, near_inv, far_inv)[rows:]))
        scales.append(CLIP_NORM / (jnp.sqrt(as_row(squared)) + 0.01))
        normed.append((ref[...].astype(F32) * inv_col * gain_ref[...]).astype(BF16))
    normed = jnp.concatenate(normed, axis=0)
    group_rows, n_groups = out_ref.shape[:2]
    step = max(1, group_rows // 4)
    for i in range(0, group_rows, step):
        rows_now = slice(i * n_groups, (i + step) * n_groups)
        clipped = jnp.concatenate(
            [
                (ref[rows_now, :].astype(F32) * scale).astype(BF16)
                for ref, scale in zip((turned_ref, turned_other_ref), scales)
            ],
            axis=1,
        )
        grad = jnp.dot(clipped, normed, preferred_element_type=F32).astype(BF16)
        out_ref[i : i + step] = grad.reshape(step, n_groups, half)


def back_kernel(
    n_y, n_x, masks, place_ref, first, second, third, last, weight_ref, input_ref, gain_ref, out_ref, inner_ref
):
    lanes = first.shape[2]
    tokens, width = input_ref.shape
    n_rows = weight_ref.shape[0]
    group_rows = n_rows // (n_y * n_x) // 4
    col = lax.broadcasted_iota(jnp.int32, (lanes, n_rows), 1)
    lane = lax.broadcasted_iota(jnp.int32, (lanes, n_rows), 0)

    def came(index, mine):
        turn = index ^ mine
        return (turn & 2) | ((turn & 1) ^ (turn >> 1))

    places = []
    for block in true_blocks(place_ref, masks):
        kv = block * lanes + lane
        row, group = kv % group_rows, kv // group_rows
        core, x, y = came(group % 2, place_ref[1]), (group // 2) % n_x, (group // (2 * n_x)) % n_y
        zh = came(group // (2 * n_x * n_y), place_ref[2])
        target = (((core * n_y + y) * n_x + x) * 2 + zh) * group_rows + row
        places.append(jnp.where(col == target, 1.0, 0.0).astype(BF16))
    places = jnp.concatenate(places, axis=0)
    cot = cot_columns((first, second, third, last), tokens)
    cot = jnp.dot(cot, places, preferred_element_type=F32).astype(BF16)
    inner = jnp.zeros((tokens, 1), F32)
    step = max(1, width // 4)
    for i in range(0, width, step):
        cols = slice(i, i + step)
        weighted = gain_ref[:, cols] * jnp.dot(cot, weight_ref[:, cols], preferred_element_type=F32)
        out_ref[:, cols] = weighted
        inner = inner + jnp.sum(weighted * input_ref[:, cols].astype(F32), axis=1, keepdims=True)
    inner_row = jnp.transpose(jnp.broadcast_to(inner, (tokens, 8)))[:1, :]
    inner_ref[...] = as_block(inner_row, lanes)


def body(
    layer_input,
    norm_gain,
    value_weight,
    value_cotangent,
    doc_ids,
    owners,
    noise_seeds,
    master,
    moment_one,
    moment_two,
):
    tokens, part_width = layer_input.shape
    cot_part = value_cotangent.shape[1]
    n_mp = lax.axis_size("mp")
    n_zh, n_core = lax.axis_size("zh"), lax.axis_size("core")
    n_yx = lax.axis_size("y") * lax.axis_size("x")
    full_width = part_width * n_mp
    group_rows = value_weight.shape[0]
    n_groups = owners.shape[0]
    value_width = n_groups * group_rows
    slots = master.shape[0] // group_rows
    half = part_width // n_core
    my_core = lax.axis_index("core")
    my_column = lax.axis_index("mp")
    my_zh = lax.axis_index("zh")
    my_yx = lax.axis_index(PLANE)
    my_group = lax.axis_index(DP_AXES)
    swap = [(0, 1), (1, 0)]

    inputs = layer_input.astype(F32)
    gain_row = norm_gain.astype(F32)[None, :]
    place = jnp.stack(
        [my_column, my_core, my_zh, lax.axis_index("y"), lax.axis_index("x")]
    ).astype(jnp.int32)

    squares_part = jnp.sum(inputs * inputs, axis=1)
    term_one = lax.reduce_precision(squares_part, 8, 7)
    rest = squares_part - term_one
    term_two = lax.reduce_precision(rest, 8, 7)
    terms = jnp.concatenate([term_one, term_two, rest - term_two]).astype(BF16)
    terms = terms.reshape(-1, cot_part)
    pad = jnp.zeros(((-terms.shape[0]) % 16, cot_part), BF16)
    packet = jnp.concatenate([value_cotangent, terms, pad], axis=0)[None]

    def across(array, bit):
        return lax.ppermute(array, "mp", [(i, i ^ bit) for i in range(n_mp)])

    top, middle = n_mp // 2, n_mp // 4
    masks = [0, top, middle, middle + top, 1, 1 + top, 1 + middle, 1 + middle + top]
    weight_far = lax.ppermute(value_weight, "zh", swap)
    input_other = lax.ppermute(
        lax.dynamic_slice(layer_input, (0, (1 - my_core) * half), (tokens, half)), "core", swap
    )
    input_own = lax.dynamic_slice(layer_input, (0, my_core * half), (tokens, half))
    doc_col, doc_row = doc_ids[:, None], doc_ids[None, :]
    packet_far = across(packet, top)
    packet_far, weight_far, input_own, input_other, doc_col, place = lax.optimization_barrier(
        (packet_far, weight_far, input_own, input_other, doc_col, place)
    )
    first = jnp.concatenate([packet, packet_far], axis=0)
    second, third = across(first, middle), across(first, 1)
    gained = (inputs * gain_row).astype(BF16)
    gram_features = jnp.dot(gained, gained.T, preferred_element_type=F32)
    second, third, gram_features = lax.optimization_barrier((second, third, gram_features))
    last = across(second, 1)

    weight_pair = jnp.concatenate([value_weight, weight_far], axis=0)
    weight_own = lax.all_to_all(
        jnp.broadcast_to(weight_pair[None], (n_yx,) + weight_pair.shape), PLANE, 0, 0
    ).reshape(value_width // n_core, part_width)
    full_weight = jnp.concatenate([weight_own, lax.ppermute(weight_own, "core", swap)], axis=0)

    rows = tokens // cot_part
    sums_packet, inv_rms = local_kernel(
        functools.partial(sums_kernel, full_width),
        (
            jax.ShapeDtypeStruct((n_core * n_mp, 2 * rows, cot_part), F32),
            jax.ShapeDtypeStruct((rows, cot_part), F32),
        ),
        2 * tokens * tokens * value_width,
        place,
        first,
        second,
        third,
        last,
        gram_features,
        doc_col,
        doc_row,
    )
    sums_all = lax.all_to_all(sums_packet, ("core", "mp"), 0, 0)
    last, inv_rms = lax.optimization_barrier((last, inv_rms))
    turned = local_kernel(
        functools.partial(turn_kernel, group_rows, masks),
        jax.ShapeDtypeStruct((value_width, tokens), BF16),
        2 * tokens * value_width * value_width,
        place,
        first,
        second,
        third,
        last,
    )
    turned_other = lax.ppermute(turned, "core", swap)
    sums_all, turned, turned_other = lax.optimization_barrier((sums_all, turned, turned_other))

    grad_rows = local_kernel(
        grad_kernel,
        jax.ShapeDtypeStruct((group_rows, n_groups, half), BF16),
        4 * tokens * value_width * half,
        place,
        sums_all,
        turned,
        turned_other,
        input_own,
        input_other,
        lax.dynamic_slice(gain_row, (0, my_core * half), (1, half)),
    )
    grad_rows, last = lax.optimization_barrier((grad_rows, last))
    weighted, inner_sum = local_kernel(
        functools.partial(back_kernel, lax.axis_size("y"), lax.axis_size("x"), masks),
        (
            jax.ShapeDtypeStruct((tokens, part_width), F32),
            jax.ShapeDtypeStruct((rows, cot_part), F32),
        ),
        4 * tokens * value_width * part_width,
        place,
        first,
        second,
        third,
        last,
        full_weight,
        layer_input,
        gain_row,
    )
    grad_rows = lax.all_to_all(grad_rows, PLANE, 0, 0)
    for bit in (1, middle):
        inner_sum = inner_sum + across(inner_sum, bit)
    grad_rows, inner_sum = lax.optimization_barrier((grad_rows, inner_sum))
    inner_sum = inner_sum + across(inner_sum, top)
    inv_col = inv_rms.reshape(tokens, 1)
    input_grad = (
        inv_col * weighted
        - inputs * inv_col * inv_col * inv_col * (inner_sum.reshape(tokens, 1) / full_width)
    ).astype(BF16)

    grad_plane = jnp.sum(grad_rows.astype(F32), axis=0)
    col_pos = my_column * part_width + my_core * half + jnp.arange(half, dtype=jnp.int32)[None, :]
    noise = gauss_noise(noise_seeds[:, None], my_yx * full_width + col_pos)
    noisy = grad_plane + jnp.where(my_zh == 0, NOISE_MULT * CLIP_NORM, 0.0) * noise

    group_ids = jnp.arange(n_groups, dtype=jnp.int32)
    earlier = group_ids[:, None] > group_ids[None, :]
    same_owner = owners[:, None] == owners[None, :]
    slot_rank = jnp.sum((earlier & same_owner).astype(jnp.int32), axis=1)
    target = owners * slots + slot_rank
    places = jnp.arange(n_groups * slots, dtype=jnp.int32)
    sends = (places[:, None] == target[None, :]).astype(F32)
    outgoing = jnp.dot(sends, noisy, precision=lax.Precision.HIGHEST).astype(BF16)
    arrived = lax.all_to_all(outgoing.reshape(n_groups, slots, half), DP_AXES, 0, 0)
    gathered = (
        jnp.sum(arrived.reshape(n_zh, n_yx, n_core, slots, half).astype(F32), axis=0)
        .transpose(2, 0, 1, 3)
        .reshape(slots * group_rows, part_width)
    )
    slot_ids = jnp.arange(slots, dtype=jnp.int32)
    filled = jnp.any(
        (owners[None, :] == my_group) & (slot_rank[None, :] == slot_ids[:, None]), axis=1
    )
    keep_mask = jnp.repeat(filled, group_rows)[:, None]
    first_new = BETA_ONE * moment_one + (1.0 - BETA_ONE) * gathered
    second_new = BETA_TWO * moment_two + (1.0 - BETA_TWO) * gathered * gathered
    update = (
        first_new
        / (1.0 - BETA_ONE**ADAM_STEP)
        / (jnp.sqrt(second_new / (1.0 - BETA_TWO**ADAM_STEP)) + ADAM_EPS)
    )
    new_master = jnp.where(keep_mask, master - LEARN_RATE * update, master)
    new_moment_one = jnp.where(keep_mask, first_new, moment_one)
    new_moment_two = jnp.where(keep_mask, second_new, moment_two)
    return (input_grad, new_master, new_moment_one, new_moment_two)


def solution(mesh, dp_split=DP_SPLIT):
    fine = Mesh(mesh.devices.reshape(dp_split + (mesh.shape["mp"],)), DP_AXES + ("mp",))
    rows, both = P(DP_AXES), P(DP_AXES, "mp")
    in_specs = (both, P("mp"), both, both, rows, P(), P(), both, both, both)
    out_specs = (both, both, both, both)
    return jax.shard_map(body, mesh=fine, in_specs=in_specs, out_specs=out_specs, check_vma=False)
```
